256 devices in a mesh: row: 16 (over z, core), col: 16 (over y, x).
Axes of the slice: x: 4, y: 4, z: 8, core: 2. Of those that a mesh axis runs over, the one named last changes fastest.
Arguments:
- vectors: float32 [2048, 48, 512], P(('row', 'col')), may hold values from -6 to 6
- factor_one: float32 [2048, 47, 2048], P('row', None, 'col'), may hold values from -0.125 to 0.125
- factor_two: float32 [2048, 46, 2048], P('row', None, 'col'), may hold values from -0.125 to 0.125
- block_inverse: float32 [2, 2048, 2048], P(None, 'row', 'col'), may hold values from -1 to 2, as said below
- lumped_mass: float32 [2048, 48], P(('row', 'col')), may hold values from 0.25 to 9.5
Outputs:
- solved: float32 [2048, 48, 512], P(('row', 'col'))
- rotated: float32 [2048, 48, 512], P(('row', 'col'))
The draws below stay inside these ranges and needn't reach their ends.
Inputs may be any that keep to these rules, and one draw needn't show every extreme that they name: Each block of block_inverse is lower triangular with diagonal entries between 0.5 and 2.
All inputs are finite; a program needn't handle non-finite values.
Results may differ from the reference program's by a relative error of at most 0.00013.
Values sent between devices are 32-bit elements; how exact they have to be, the bound alone decides.
No kernel may reach another device: no remote copies, remote signals or barrier semaphores. Data moves between devices by JAX's collectives and lax.ppermute only.
A program may use at most 128 MiB of HBM per device.

```python
import math
import jax
import jax.numpy as jnp
from jax import lax

PW = 2048
K = 512
ROUNDS = 48
PANELS = 2
ORDER = 98304


def draw_block_inverse(key, part):
    key_diag, key_off = jax.random.split(jax.random.fold_in(key, 11))
    shape = (PANELS, PW, PW)
    rows_index = lax.broadcasted_iota(jnp.int32, shape, 1)
    cols_index = lax.broadcasted_iota(jnp.int32, shape, 2)
    diagonal = jax.random.uniform(key_diag, shape, jnp.float32, 0.6, 1.6)
    offdiag = jnp.clip(jax.random.normal(key_off, shape, jnp.float32), -6.0, 6.0)
    offdiag = offdiag * (0.5 / math.sqrt(PW))
    lower_part = jnp.where(cols_index < rows_index, offdiag, 0.0)
    return jnp.where(rows_index == cols_index, diagonal, lower_part)


def draw_lumped_mass(key, part):
    shape = (PW, ROUNDS)
    ramp_up = 1.0 + 2.0 * lax.broadcasted_iota(jnp.float32, shape, 0) / PW
    rough = jnp.exp(jax.random.uniform(jax.random.fold_in(key, 23), shape, jnp.float32, math.log(0.5), math.log(2.0)))
    return ramp_up * rough


def levels(key, dims, cuts, least, high):
    gain = 1.0
    for axis_at, blocks in cuts:
        heights = jax.random.uniform(jax.random.fold_in(jax.random.fold_in(key, 6), axis_at), (blocks,), jnp.float32, least / len(cuts), high / len(cuts))
        gain = gain * jnp.repeat(jnp.exp(heights), dims[axis_at] // blocks).reshape((-1,) + (1,) * (len(dims) - 1 - axis_at))
    return gain


def gaussian(rng, extent, spread, most, shards=(), dtype=jnp.bfloat16):
    result = jax.random.normal(rng, extent, jnp.float32) * spread
    if len(shards) > 0:
        result = levels(rng, extent, shards, -0.22, 0.18) * result
    return jnp.clip(result, min=-most, max=most).astype(dtype)


def setup_inputs(seed: int = 0) -> dict:
    key_list = jax.random.split(jax.random.key(seed), 6)
    vectors = gaussian(key_list[0], (PW, ROUNDS, K), 1.0, 6.0, ((0, 256),), jnp.float32)
    factor_one = gaussian(key_list[1], (PW, ROUNDS - 1, PW), PW ** -0.5, 0.125, ((0, 16), (2, 16)), jnp.float32)
    factor_two = gaussian(key_list[2], (PW, ROUNDS - 2, PW), PW ** -0.5, 0.125, ((0, 16), (2, 16)), jnp.float32)
    block_inverse = draw_block_inverse(jax.random.fold_in(key_list[5], 71), 0)
    lumped_mass = draw_lumped_mass(jax.random.fold_in(key_list[5], 71), 0)
    return {"vectors": vectors, "factor_one": factor_one, "factor_two": factor_two, "block_inverse": block_inverse, "lumped_mass": lumped_mass}


def reference(vectors, factor_one, factor_two, block_inverse, lumped_mass):
    highest = lax.Precision.HIGHEST
    panel_one = jnp.dot(block_inverse[0].astype(jnp.float32), vectors[:, 0, :].astype(jnp.float32), precision=highest, preferred_element_type=jnp.float32)
    remain = vectors[:, 1:, :] - jnp.einsum('jtq,qk->jtk', factor_one, panel_one, precision=highest)
    panel_two = jnp.dot(block_inverse[1].astype(jnp.float32), remain[:, 0, :].astype(jnp.float32), precision=highest, preferred_element_type=jnp.float32)
    remaining = remain[:, 1:, :] - jnp.einsum('jtq,qk->jtk', factor_two, panel_two, precision=highest)
    solved = jnp.concatenate([panel_one[:, None, :], panel_two[:, None, :], remaining], axis=1)
    weighted = solved * lumped_mass[:, :, None]
    mass_gram = jnp.einsum('jtk,jtl->kl', weighted, solved, precision=highest) / ORDER
    factor = jnp.linalg.cholesky(mass_gram)
    flattened = solved.reshape(-1, solved.shape[2])
    rotated = jax.scipy.linalg.solve_triangular(factor, flattened.T, lower=True).T
    return (solved, rotated.reshape(solved.shape))
```

```python
import jax
import jax.numpy as jnp
from jax import lax
from jax.sharding import PartitionSpec as P

ORDER = 98304
HIGHEST = lax.Precision.HIGHEST


def exchange(blocks, axis):
    return lax.all_to_all(blocks, axis, 0, 0)


def share(block, axis):
    size = lax.axis_size(axis)
    return exchange(jnp.broadcast_to(block[None], (size,) + block.shape), axis)


def product(rows, tiles):
    return jnp.einsum("rkq,riq->ki", rows, tiles, precision=HIGHEST, preferred_element_type=jnp.float32)


def trailing(factor, panel):
    out = jnp.einsum("rjtq,crkq->jtck", factor, panel, precision=HIGHEST, preferred_element_type=jnp.float32)
    return out.reshape(out.shape[:2] + (-1,))


def body(vectors, factor_one, factor_two, block_inverse, lumped_mass):
    rows_n, cols_n = lax.axis_size("row"), lax.axis_size("col")
    row, col = lax.axis_index("row"), lax.axis_index("col")
    core, place = row % 2, row // 2
    own, rounds, k_all = vectors.shape
    tile = own * cols_n
    k_part = k_all // cols_n
    swap = [(i, i ^ 1) for i in range(rows_n)]

    heads = vectors[:, :2, :].reshape(own, 2, cols_n, k_part).transpose(2, 1, 0, 3)
    heads = exchange(heads, "col")
    heads = heads.transpose(1, 3, 0, 2).reshape(2, k_part, tile)
    head_rows = share(heads[0], "row")

    mats = jnp.stack([block_inverse[0], factor_one[:, 0, :], block_inverse[1]])
    mats = share(mats, "col")

    def whole(panel_rows):
        mine = lax.dynamic_index_in_dim(
            panel_rows.reshape((rows_n // 2, 2) + panel_rows.shape[1:]), core, 1, keepdims=False
        )
        mine = share(mine, "col")
        return mine, lax.ppermute(mine, "row", swap)

    def owned(mine):
        block = lax.dynamic_index_in_dim(mine, place, 1, keepdims=False)
        block = lax.dynamic_slice_in_dim(block, col * own, own, 2)
        return block.transpose(2, 0, 1).reshape(own, k_all)

    def halves(factor):
        parts = exchange(factor.reshape((cols_n, own) + factor.shape[1:]), "col")
        parts = parts.reshape((rows_n // 2, 2) + parts.shape[1:])
        return (
            lax.dynamic_index_in_dim(parts, core, 1, keepdims=False),
            lax.dynamic_index_in_dim(parts, 1 - core, 1, keepdims=False),
        )

    one_rows = share(product(head_rows, mats[:, 0]), "row")
    remain_head = heads[1] - product(one_rows, mats[:, 1])
    remain_rows = share(remain_head, "row")
    two_rows = share(product(remain_rows, mats[:, 2]), "row")

    one_mine, one_other = whole(one_rows)
    f_mine, f_other = halves(factor_one)
    remain = vectors[:, 1:, :] - trailing(f_mine, one_mine) - trailing(f_other, one_other)

    two_mine, two_other = whole(two_rows)
    f_mine, f_other = halves(factor_two)
    remaining = remain[:, 1:, :] - trailing(f_mine, two_mine) - trailing(f_other, two_other)

    solved = jnp.concatenate([owned(one_mine)[:, None, :], owned(two_mine)[:, None, :], remaining], axis=1)
    weighted = solved * lumped_mass[:, :, None]
    gram = jnp.einsum("jtk,jtl->kl", weighted, solved, precision=HIGHEST, preferred_element_type=jnp.float32)

    lanes = k_all // 4
    gram = gram.reshape(cols_n, 4, own, 4, lanes).transpose(0, 1, 3, 2, 4)
    gram = exchange(gram, "col").sum(axis=0)
    gram = exchange(gram.reshape(rows_n, own, lanes), "row").sum(axis=0)
    gram = share(share(gram, "row"), "col")
    gram = gram.reshape(cols_n, 4, 4, own, lanes).transpose(0, 1, 3, 2, 4).reshape(k_all, k_all)

    factor = jnp.linalg.cholesky(gram / ORDER)
    flattened = solved.reshape(-1, k_all)
    rotated = jax.scipy.linalg.solve_triangular(factor, flattened.T, lower=True).T
    return (solved, rotated.reshape(solved.shape))


def solution(mesh):
    placed = (
        P(("row", "col"), None, None),
        P("row", None, "col"),
        P("row", None, "col"),
        P(None, "row", "col"),
        P(("row", "col"), None),
    )
    return jax.shard_map(
        body,
        mesh=mesh,
        in_specs=placed,
        out_specs=(P(("row", "col"), None, None), P(("row", "col"), None, None)),
        check_vma=False,
    )
```

```python
import functools
import jax
import jax.numpy as jnp
from jax import lax
from jax.experimental import pallas as pl
from jax.experimental.pallas import tpu as pltpu
from jax.sharding import PartitionSpec as P

ORDER = 98304
HIGHEST = lax.Precision.HIGHEST


G=8
def small_dot(a,b,ca,cb):
    return lax.dot_general(a,b,(((ca,),(cb,)),((),())),precision=HIGHEST,preferred_element_type=jnp.float32)

def invert_block(a_ref, b_ref):
    n=a_ref.shape[0]
    full=(G,n)
    for g in range(n//G):
        lo=g*G
        block=a_ref[lo:lo+G,:]
        d={(i,j): jnp.broadcast_to(block[i:i+1,lo+j:lo+j+1],full) for i in range(G) for j in range(i+1)}
        a=[jnp.broadcast_to(block[j:j+1,:],full) for j in range(G)]
        bb=b_ref[lo:lo+G,:]
        b=[jnp.broadcast_to(bb[j:j+1,:],full) for j in range(G)]
        r={}
        for j in range(G):
            r[j]=lax.rsqrt(d[j,j])
            for i in range(j+1,G):
                d[i,j]=d[i,j]*r[j]
            for i in range(j+1,G):
                for k in range(i,G):
                    d[k,i]=d[k,i]-d[k,j]*d[i,j]
            a[j]=a[j]*r[j]; b[j]=b[j]*r[j]
            for i in range(j+1,G):
                a[i]=a[i]-d[i,j]*a[j]; b[i]=b[i]-d[i,j]*b[j]
        sub=lax.broadcasted_iota(jnp.int32,full,0)
        outb=b[0]
        for j in range(1,G): outb=jnp.where(sub==j,b[j],outb)
        b_ref[lo:lo+G,:]=outb
        for h in range(g+1,n//G):
            hs=slice(h*G,h*G+G)
            ah=a_ref[hs,:]; bh=b_ref[hs,:]
            c=[jnp.broadcast_to(ah[:,lo+j:lo+j+1],full) for j in range(G)]
            for j in range(G):
                c[j]=c[j]*r[j]
                for i in range(j+1,G):
                    c[i]=c[i]-d[i,j]*c[j]
                ah=ah-c[j]*a[j]; bh=bh-c[j]*b[j]
            a_ref[hs,:]=ah; b_ref[hs,:]=bh

def kernel(scale, gram_ref, out_ref, a_ref, s_ref, t_ref):
    n=gram_ref.shape[0]; nb=128
    a_ref[...]=gram_ref[...]*scale
    out_ref[...]=jnp.where(lax.broadcasted_iota(jnp.int32,(n,n),0)==lax.broadcasted_iota(jnp.int32,(n,n),1),1.0,0.0)
    def one(b,_):
        at=pl.multiple_of(b*nb,nb)
        rows=pl.ds(at,nb)
        s_ref[...]=a_ref[rows,rows]
        t_ref[...]=jnp.where(lax.broadcasted_iota(jnp.int32,(nb,nb),0)==lax.broadcasted_iota(jnp.int32,(nb,nb),1),1.0,0.0)
        invert_block(s_ref,t_ref)
        inv=t_ref[...]
        u=small_dot(inv,a_ref[rows,:],1,0)
        x=small_dot(inv,out_ref[rows,:],1,0)
        out_ref[rows,:]=x
        below=lax.broadcasted_iota(jnp.int32,(nb,n),1)>=at+nb
        uu=jnp.where(below,u,0.0)
        def rest(i,_):
            r2=pl.ds(pl.multiple_of(i*nb,nb),nb)
            ui=small_dot(inv,a_ref[rows,r2],1,0)
            a_ref[r2,:]=a_ref[r2,:]-small_dot(ui,uu,0,0)
            out_ref[r2,:]=out_ref[r2,:]-small_dot(ui,x,0,0)
            return 0
        lax.fori_loop(b+1,n//nb,rest,0)
        return 0
    lax.fori_loop(0,n//nb,one,0)

def inverse_factor(gram, scale):
    n=gram.shape[0]
    return pl.pallas_call(functools.partial(kernel,scale),
        out_shape=jax.ShapeDtypeStruct((n,n),jnp.float32),
        in_specs=[pl.BlockSpec(memory_space=pltpu.VMEM)],
        out_specs=pl.BlockSpec(memory_space=pltpu.VMEM),
        scratch_shapes=[pltpu.VMEM((n,n),jnp.float32),pltpu.VMEM((128,128),jnp.float32),pltpu.VMEM((128,128),jnp.float32)],
        compiler_params=pltpu.CompilerParams(vmem_limit_bytes=16*1024*1024))(gram)


def exchange(blocks, axis):
    return lax.all_to_all(blocks, axis, 0, 0)


def share(block, axis):
    size = lax.axis_size(axis)
    return exchange(jnp.broadcast_to(block[None], (size,) + block.shape), axis)


def product(rows, tiles):
    return jnp.einsum("rkq,riq->ki", rows, tiles, precision=HIGHEST, preferred_element_type=jnp.float32)


def trailing(factor, panel):
    out = jnp.einsum("rjtq,crkq->jtck", factor, panel, precision=HIGHEST, preferred_element_type=jnp.float32)
    return out.reshape(out.shape[:2] + (-1,))


def body(vectors, factor_one, factor_two, block_inverse, lumped_mass):
    rows_n, cols_n = lax.axis_size("row"), lax.axis_size("col")
    row, col = lax.axis_index("row"), lax.axis_index("col")
    core, place = row % 2, row // 2
    own, rounds, k_all = vectors.shape
    tile = own * cols_n
    k_part = k_all // cols_n
    swap = [(i, i ^ 1) for i in range(rows_n)]

    heads = vectors[:, :2, :].reshape(own, 2, cols_n, k_part).transpose(2, 1, 0, 3)
    heads = exchange(heads, "col")
    heads = heads.transpose(1, 3, 0, 2).reshape(2, k_part, tile)
    head_rows = share(heads[0], "row")

    mats = jnp.stack([block_inverse[0], factor_one[:, 0, :], block_inverse[1]])
    mats = lax.all_gather(mats, "col")

    def whole(panel_rows):
        mine = lax.dynamic_index_in_dim(
            panel_rows.reshape((rows_n // 2, 2) + panel_rows.shape[1:]), core, 1, keepdims=False
        )
        mine = lax.all_gather(mine, "col")
        return mine, lax.ppermute(mine, "row", swap)

    def owned(mine):
        block = lax.dynamic_index_in_dim(mine, place, 1, keepdims=False)
        block = lax.dynamic_slice_in_dim(block, col * own, own, 2)
        return block.transpose(2, 0, 1).reshape(own, k_all)

    def halves(factor):
        parts = exchange(factor.reshape((cols_n, own) + factor.shape[1:]), "col")
        parts = parts.reshape((rows_n // 2, 2) + parts.shape[1:])
        return (
            lax.dynamic_index_in_dim(parts, core, 1, keepdims=False),
            lax.dynamic_index_in_dim(parts, 1 - core, 1, keepdims=False),
        )

    f_one = halves(factor_one)
    mats, f_one = lax.optimization_barrier((mats, f_one))
    one_rows = share(product(head_rows, mats[:, 0]), "row")
    one_mine, one_other = whole(one_rows)
    remain_head = heads[1] - product(one_rows, mats[:, 1])
    remain_rows = share(remain_head, "row")
    two_rows = share(product(remain_rows, mats[:, 2]), "row")
    two_mine, two_other = whole(two_rows)
    f_two = halves(factor_two)
    remain = vectors[:, 1:, :] - trailing(f_one[0], one_mine) - trailing(f_one[1], one_other)
    remaining = remain[:, 1:, :] - trailing(f_two[0], two_mine) - trailing(f_two[1], two_other)

    solved = jnp.concatenate([owned(one_mine)[:, None, :], owned(two_mine)[:, None, :], remaining], axis=1)
    weighted = solved * lumped_mass[:, :, None]
    gram = jnp.einsum("jtk,jtl->kl", weighted, solved, precision=HIGHEST, preferred_element_type=jnp.float32)

    lanes = k_all // 4
    gram = gram.reshape(cols_n, 4, own, 4, lanes).transpose(0, 1, 3, 2, 4)
    gram = exchange(gram, "col").sum(axis=0)
    gram = exchange(gram.reshape(rows_n, own, lanes), "row").sum(axis=0)
    gram = share(share(gram, "row"), "col")
    gram = gram.reshape(cols_n, 4, 4, own, lanes).transpose(0, 1, 3, 2, 4).reshape(k_all, k_all)

    inverse = inverse_factor(gram, 1.0 / ORDER)
    rotated = jnp.einsum("jtk,lk->jtl", solved, inverse, precision=HIGHEST, preferred_element_type=jnp.float32)
    return (solved, rotated)


def solution(mesh):
    placed = (
        P(("row", "col"), None, None),
        P("row", None, "col"),
        P("row", None, "col"),
        P(None, "row", "col"),
        P(("row", "col"), None),
    )
    return jax.shard_map(
        body,
        mesh=mesh,
        in_specs=placed,
        out_specs=(P(("row", "col"), None, None), P(("row", "col"), None, None)),
        check_vma=False,
    )
```

```python
import functools
import jax
import jax.numpy as jnp
from jax import lax
from jax.experimental import pallas as pl
from jax.experimental.pallas import tpu as pltpu
from jax.sharding import PartitionSpec as P

ORDER = 98304
HIGHEST = lax.Precision.HIGHEST


PIVOTS = 8
BLOCK = 128


def small_dot(a, b, a_dim, b_dim):
    return lax.dot_general(
        a, b, (((a_dim,), (b_dim,)), ((), ())), precision=HIGHEST, preferred_element_type=jnp.float32
    )


def identity(n):
    rows = lax.broadcasted_iota(jnp.int32, (n, n), 0)
    return jnp.where(rows == lax.broadcasted_iota(jnp.int32, (n, n), 1), 1.0, 0.0)


def invert_block(a_ref, b_ref):
    n = a_ref.shape[0]
    full = (PIVOTS, n)
    for lo in range(0, n, PIVOTS):
        block = a_ref[lo : lo + PIVOTS, :]
        other = b_ref[lo : lo + PIVOTS, :]
        d = {
            (i, j): jnp.broadcast_to(block[i : i + 1, lo + j : lo + j + 1], full)
            for i in range(PIVOTS)
            for j in range(i + 1)
        }
        a = [jnp.broadcast_to(block[j : j + 1, :], full) for j in range(PIVOTS)]
        b = [jnp.broadcast_to(other[j : j + 1, :], full) for j in range(PIVOTS)]
        r = {}
        for j in range(PIVOTS):
            r[j] = lax.rsqrt(d[j, j])
            for i in range(j + 1, PIVOTS):
                d[i, j] = d[i, j] * r[j]
            for i in range(j + 1, PIVOTS):
                for k in range(i, PIVOTS):
                    d[k, i] = d[k, i] - d[k, j] * d[i, j]
            a[j] = a[j] * r[j]
            b[j] = b[j] * r[j]
            for i in range(j + 1, PIVOTS):
                a[i] = a[i] - d[i, j] * a[j]
                b[i] = b[i] - d[i, j] * b[j]
        sub = lax.broadcasted_iota(jnp.int32, full, 0)
        done = b[0]
        for j in range(1, PIVOTS):
            done = jnp.where(sub == j, b[j], done)
        b_ref[lo : lo + PIVOTS, :] = done
        for at in range(lo + PIVOTS, n, PIVOTS):
            ah = a_ref[at : at + PIVOTS, :]
            bh = b_ref[at : at + PIVOTS, :]
            c = [jnp.broadcast_to(ah[:, lo + j : lo + j + 1], full) for j in range(PIVOTS)]
            for j in range(PIVOTS):
                c[j] = c[j] * r[j]
                for i in range(j + 1, PIVOTS):
                    c[i] = c[i] - d[i, j] * c[j]
                ah = ah - c[j] * a[j]
                bh = bh - c[j] * b[j]
            a_ref[at : at + PIVOTS, :] = ah
            b_ref[at : at + PIVOTS, :] = bh


def block_pairs(n):
    return [(i, j) for i in range(n // BLOCK) for j in range(i, n // BLOCK)]


def inverse_kernel(scale, core_ref, mine_ref, other_ref, out_ref, a_ref, s_ref, t_ref):
    n = out_ref.shape[0]
    pairs = block_pairs(n)
    half = len(pairs) // 2
    core = core_ref[0]
    for side in range(2):
        for at, (i, j) in enumerate(pairs[side * half : (side + 1) * half]):
            rows, cols = slice(i * BLOCK, (i + 1) * BLOCK), slice(j * BLOCK, (j + 1) * BLOCK)
            part = jnp.where(core == side, mine_ref[at], other_ref[at])
            a_ref[rows, cols] = part * scale
    out_ref[...] = identity(n)

    def one(b, _):
        at = pl.multiple_of(b * BLOCK, BLOCK)
        rows = pl.ds(at, BLOCK)
        s_ref[...] = a_ref[rows, rows]
        t_ref[...] = identity(BLOCK)
        invert_block(s_ref, t_ref)
        inv = t_ref[...]
        below = lax.broadcasted_iota(jnp.int32, (BLOCK, n), 1) >= at + BLOCK
        u = small_dot(inv, jnp.where(below, a_ref[rows, :], 0.0), 1, 0)
        x = small_dot(inv, out_ref[rows, :], 1, 0)
        out_ref[rows, :] = x

        def rest(i, _):
            later = pl.ds(pl.multiple_of(i * BLOCK, BLOCK), BLOCK)
            ui = small_dot(inv, a_ref[rows, later], 1, 0)
            a_ref[later, :] = a_ref[later, :] - small_dot(ui, u, 0, 0)
            out_ref[later, :] = out_ref[later, :] - small_dot(ui, x, 0, 0)
            return 0

        lax.fori_loop(b + 1, n // BLOCK, rest, 0)
        return 0

    lax.fori_loop(0, n // BLOCK, one, 0)


def inverse_factor(core, mine, other, n, scale):
    return pl.pallas_call(
        functools.partial(inverse_kernel, scale),
        out_shape=jax.ShapeDtypeStruct((n, n), jnp.float32),
        in_specs=[pl.BlockSpec(memory_space=pltpu.SMEM)] + [pl.BlockSpec(memory_space=pltpu.VMEM)] * 2,
        out_specs=pl.BlockSpec(memory_space=pltpu.VMEM),
        scratch_shapes=[
            pltpu.VMEM((n, n), jnp.float32),
            pltpu.VMEM((BLOCK, BLOCK), jnp.float32),
            pltpu.VMEM((BLOCK, BLOCK), jnp.float32),
        ],
        compiler_params=pltpu.CompilerParams(vmem_limit_bytes=16 * 1024 * 1024),
    )(jnp.full((1,), core, jnp.int32), mine, other)


def exchange(blocks, axis):
    return lax.all_to_all(blocks, axis, 0, 0)


def share(block, axis):
    size = lax.axis_size(axis)
    return exchange(jnp.broadcast_to(block[None], (size,) + block.shape), axis)


def product(rows, tiles):
    return jnp.einsum("rkq,riq->ki", rows, tiles, precision=HIGHEST, preferred_element_type=jnp.float32)


def trailing(factor, panel):
    out = jnp.einsum("rjtq,crkq->jtck", factor, panel, precision=HIGHEST, preferred_element_type=jnp.float32)
    return out.reshape(out.shape[:2] + (-1,))


def body(vectors, factor_one, factor_two, block_inverse, lumped_mass):
    rows_n, cols_n = lax.axis_size("row"), lax.axis_size("col")
    row, col = lax.axis_index("row"), lax.axis_index("col")
    core, place = row % 2, row // 2
    own, rounds, k_all = vectors.shape
    tile = own * cols_n
    k_part = k_all // cols_n
    swap = [(i, i ^ 1) for i in range(rows_n)]

    heads = vectors[:, :2, :].reshape(own, 2, cols_n, k_part).transpose(2, 1, 0, 3)
    heads = exchange(heads, "col")
    heads = heads.transpose(1, 3, 0, 2).reshape(2, k_part, tile)
    head_rows = share(heads[0], "row")

    mats = jnp.stack([block_inverse[0], factor_one[:, 0, :], block_inverse[1]])
    mats = lax.all_gather(mats, "col")

    def gather_half(panel_rows):
        mine = lax.dynamic_index_in_dim(
            panel_rows.reshape((rows_n // 2, 2) + panel_rows.shape[1:]), core, 1, keepdims=False
        )
        return lax.all_gather(mine, "col")

    def owned(mine):
        block = lax.dynamic_index_in_dim(mine, place, 1, keepdims=False)
        block = lax.dynamic_slice_in_dim(block, col * own, own, 2)
        return block.transpose(2, 0, 1).reshape(own, k_all)

    def halves(factor):
        parts = exchange(factor.reshape((cols_n, own) + factor.shape[1:]), "col")
        parts = parts.reshape((rows_n // 2, 2) + parts.shape[1:])
        return (
            lax.dynamic_index_in_dim(parts, core, 1, keepdims=False),
            lax.dynamic_index_in_dim(parts, 1 - core, 1, keepdims=False),
        )

    f_one = halves(factor_one)
    mats, f_one = lax.optimization_barrier((mats, f_one))
    one_rows = share(product(head_rows, mats[:, 0]), "row")
    one_mine = gather_half(one_rows)
    one_other = lax.ppermute(one_mine, "row", swap)
    remain_head = heads[1] - product(one_rows, mats[:, 1])
    remain_rows = share(remain_head, "row")
    two_rows = share(product(remain_rows, mats[:, 2]), "row")
    two_mine = gather_half(two_rows)
    f_two = halves(factor_two)
    remain = vectors[:, 1:, :] - trailing(f_one[0], one_mine) - trailing(f_one[1], one_other)
    remain, two_mine = lax.optimization_barrier((remain, two_mine))
    two_other = lax.ppermute(two_mine, "row", swap)
    remaining = remain[:, 1:, :] - trailing(f_two[0], two_mine) - trailing(f_two[1], two_other)

    solved = jnp.concatenate([owned(one_mine)[:, None, :], owned(two_mine)[:, None, :], remaining], axis=1)
    weighted = solved * lumped_mass[:, :, None]
    gram = jnp.einsum("jtk,jtl->kl", weighted, solved, precision=HIGHEST, preferred_element_type=jnp.float32)

    blocks = jnp.stack(
        [gram[i * BLOCK : (i + 1) * BLOCK, j * BLOCK : (j + 1) * BLOCK] for i, j in block_pairs(k_all)]
    )
    blocks = blocks.reshape((2, -1, BLOCK))
    there = lax.ppermute(lax.dynamic_index_in_dim(blocks, 1 - core, 0, keepdims=False), "row", swap)
    part = lax.dynamic_index_in_dim(blocks, core, 0, keepdims=False) + there
    part = exchange(part.reshape(cols_n, -1, BLOCK), "col").sum(axis=0)
    step = 2
    while step < rows_n:
        part = part + lax.ppermute(part, "row", [(i, i ^ step) for i in range(rows_n)])
        step *= 2
    mine = share(part, "col").reshape(-1, BLOCK, BLOCK)
    other = lax.ppermute(mine, "row", swap)

    inverse = inverse_factor(core, mine, other, k_all, 1.0 / ORDER)
    rotated = jnp.einsum("jtk,lk->jtl", solved, inverse, precision=HIGHEST, preferred_element_type=jnp.float32)
    return (solved, rotated)


def solution(mesh):
    placed = (
        P(("row", "col"), None, None),
        P("row", None, "col"),
        P("row", None, "col"),
        P(None, "row", "col"),
        P(("row", "col"), None),
    )
    return jax.shard_map(
        body,
        mesh=mesh,
        in_specs=placed,
        out_specs=(P(("row", "col"), None, None), P(("row", "col"), None, None)),
        check_vma=False,
    )
```

```python
import functools
import jax
import jax.numpy as jnp
from jax import lax
from jax.experimental import pallas as pl
from jax.experimental.pallas import tpu as pltpu
from jax.sharding import PartitionSpec as P

ORDER = 98304
HIGHEST = lax.Precision.HIGHEST


PIVOTS = 8
BLOCK = 128


def small_dot(a, b, a_dim, b_dim):
    return lax.dot_general(
        a, b, (((a_dim,), (b_dim,)), ((), ())), precision=HIGHEST, preferred_element_type=jnp.float32
    )


def identity(n):
    rows = lax.broadcasted_iota(jnp.int32, (n, n), 0)
    return jnp.where(rows == lax.broadcasted_iota(jnp.int32, (n, n), 1), 1.0, 0.0)


def invert_block(a_ref, b_ref):
    n = a_ref.shape[0]
    full = (PIVOTS, n)
    for lo in range(0, n, PIVOTS):
        block = a_ref[lo : lo + PIVOTS, :]
        other = b_ref[lo : lo + PIVOTS, :]
        d = {
            (i, j): jnp.broadcast_to(block[i : i + 1, lo + j : lo + j + 1], full)
            for i in range(PIVOTS)
            for j in range(i + 1)
        }
        a = [jnp.broadcast_to(block[j : j + 1, :], full) for j in range(PIVOTS)]
        b = [jnp.broadcast_to(other[j : j + 1, :], full) for j in range(PIVOTS)]
        r = {}
        for j in range(PIVOTS):
            r[j] = lax.rsqrt(d[j, j])
            for i in range(j + 1, PIVOTS):
                d[i, j] = d[i, j] * r[j]
            for i in range(j + 1, PIVOTS):
                for k in range(i, PIVOTS):
                    d[k, i] = d[k, i] - d[k, j] * d[i, j]
            a[j] = a[j] * r[j]
            b[j] = b[j] * r[j]
            for i in range(j + 1, PIVOTS):
                a[i] = a[i] - d[i, j] * a[j]
                b[i] = b[i] - d[i, j] * b[j]
        sub = lax.broadcasted_iota(jnp.int32, full, 0)
        done = b[0]
        for j in range(1, PIVOTS):
            done = jnp.where(sub == j, b[j], done)
        b_ref[lo : lo + PIVOTS, :] = done
        for at in range(lo + PIVOTS, n, PIVOTS):
            ah = a_ref[at : at + PIVOTS, :]
            bh = b_ref[at : at + PIVOTS, :]
            c = [jnp.broadcast_to(ah[:, lo + j : lo + j + 1], full) for j in range(PIVOTS)]
            for j in range(PIVOTS):
                c[j] = c[j] * r[j]
                for i in range(j + 1, PIVOTS):
                    c[i] = c[i] - d[i, j] * c[j]
                ah = ah - c[j] * a[j]
                bh = bh - c[j] * b[j]
            a_ref[at : at + PIVOTS, :] = ah
            b_ref[at : at + PIVOTS, :] = bh


def block_pairs(n):
    return [(i, j) for i in range(n // BLOCK) for j in range(i, n // BLOCK)]


def inverse_kernel(scale, core_ref, mine_ref, other_ref, out_ref, a_ref, s_ref, t_ref):
    n = out_ref.shape[0]
    pairs = block_pairs(n)
    half = len(pairs) // 2
    core = core_ref[0]
    for side in range(2):
        for at, (i, j) in enumerate(pairs[side * half : (side + 1) * half]):
            rows, cols = slice(i * BLOCK, (i + 1) * BLOCK), slice(j * BLOCK, (j + 1) * BLOCK)
            part = jnp.where(core == side, mine_ref[at], other_ref[at])
            a_ref[rows, cols] = part * scale
    out_ref[...] = identity(n)

    def one(b, _):
        at = pl.multiple_of(b * BLOCK, BLOCK)
        rows = pl.ds(at, BLOCK)
        s_ref[...] = a_ref[rows, rows]
        t_ref[...] = identity(BLOCK)
        invert_block(s_ref, t_ref)
        inv = t_ref[...]
        below = lax.broadcasted_iota(jnp.int32, (BLOCK, n), 1) >= at + BLOCK
        u = small_dot(inv, jnp.where(below, a_ref[rows, :], 0.0), 1, 0)
        x = small_dot(inv, out_ref[rows, :], 1, 0)
        out_ref[rows, :] = x

        def rest(i, _):
            later = pl.ds(pl.multiple_of(i * BLOCK, BLOCK), BLOCK)
            ui = small_dot(inv, a_ref[rows, later], 1, 0)
            a_ref[later, :] = a_ref[later, :] - small_dot(ui, u, 0, 0)
            out_ref[later, :] = out_ref[later, :] - small_dot(ui, x, 0, 0)
            return 0

        lax.fori_loop(b + 1, n // BLOCK, rest, 0)
        return 0

    lax.fori_loop(0, n // BLOCK, one, 0)


def inverse_factor(core, mine, other, n, scale):
    return pl.pallas_call(
        functools.partial(inverse_kernel, scale),
        out_shape=jax.ShapeDtypeStruct((n, n), jnp.float32),
        in_specs=[pl.BlockSpec(memory_space=pltpu.SMEM)] + [pl.BlockSpec(memory_space=pltpu.VMEM)] * 2,
        out_specs=pl.BlockSpec(memory_space=pltpu.VMEM),
        scratch_shapes=[
            pltpu.VMEM((n, n), jnp.float32),
            pltpu.VMEM((BLOCK, BLOCK), jnp.float32),
            pltpu.VMEM((BLOCK, BLOCK), jnp.float32),
        ],
        compiler_params=pltpu.CompilerParams(vmem_limit_bytes=16 * 1024 * 1024),
    )(jnp.full((1,), core, jnp.int32), mine, other)


def exchange(blocks, axis):
    return lax.all_to_all(blocks, axis, 0, 0)


def share(block, axis):
    size = lax.axis_size(axis)
    return exchange(jnp.broadcast_to(block[None], (size,) + block.shape), axis)


def sent(block, axis, shift):
    size = lax.axis_size(axis)
    return lax.ppermute(block, axis, [(i, shift(i)) for i in range(size)])


def pick(array, at, axis=0):
    return lax.dynamic_index_in_dim(array, at, axis, keepdims=False)


def gather_z(block):
    chips = lax.axis_size("row") // 2
    place = lax.axis_index("row") // 2
    out = jnp.zeros((chips,) + block.shape, block.dtype)
    out = lax.dynamic_update_index_in_dim(out, block, place, 0)
    for d in range(1, chips):
        got = sent(block, "row", lambda i: (i // 2 + d) % chips * 2 + i % 2)
        out = lax.dynamic_update_index_in_dim(out, got, (place - d) % chips, 0)
    return out


def exchange_permuted(blocks, y_first):
    side = 4
    col = lax.axis_index("col")
    y, x = col // side, col % side
    shifts = (
        lambda k: lambda i: (i // side + k) % side * side + i % side,
        lambda k: lambda i: i // side * side + (i % side + k) % side,
    )
    at = (y, x)
    first, second = (0, 1) if y_first else (1, 0)
    blocks = blocks.reshape((side, side) + blocks.shape[1:])
    stage = []
    for k in range(side):
        part = pick(blocks, (at[first] + k) % side, first)
        stage.append(sent(part, "col", shifts[first](k)) if k else part)
    done = []
    for k in range(side):
        part = jnp.stack([pick(got, (at[second] + k) % side) for got in stage])
        done.append(sent(part, "col", shifts[second](k)) if k else part)
    done = jnp.concatenate(done)
    out = []
    for source in range(side * side):
        place = (source // side, source % side)
        k1, k2 = (at[first] - place[first]) % side, (at[second] - place[second]) % side
        out.append(pick(done, k2 * side + k1))
    return jnp.stack(out)


def product(tiles, other_tiles, rows, core):
    parts = [
        jnp.einsum("ziq,kq->zki", t, rows, precision=HIGHEST, preferred_element_type=jnp.float32)
        for t in (tiles, other_tiles)
    ]
    return by_core(core, parts, 1)


def by_core(core, parts, axis):
    mine, other = parts
    return jnp.stack([jnp.where(core == 0, mine, other), jnp.where(core == 0, other, mine)], axis=axis)


def trailing(factor, panel):
    return jnp.einsum("ctjq,ckq->tjk", factor, panel, precision=HIGHEST, preferred_element_type=jnp.float32)


def body(vectors, factor_one, factor_two, block_inverse, lumped_mass):
    rows_n, cols_n = lax.axis_size("row"), lax.axis_size("col")
    row, col = lax.axis_index("row"), lax.axis_index("col")
    core, chips = row % 2, rows_n // 2
    own, rounds, k_all = vectors.shape
    tile = own * cols_n
    k_part = k_all // rows_n

    def swap(block):
        return sent(block, "row", lambda i: i ^ 1)

    heads = vectors[:, :2, :].reshape(own, 2, 2, chips, k_part).transpose(3, 2, 1, 0, 4)
    heads = exchange(heads.reshape(rows_n, 2, own, k_part), "row")
    heads = exchange(heads, "col")
    heads = heads.transpose(1, 3, 0, 2).reshape(2, k_part, tile)

    mats = gather_z(jnp.stack([block_inverse[0], factor_one[:, 0, :], block_inverse[1]]))
    other_mats = swap(mats)

    def solve(rows, which):
        out = product(mats[:, which], other_mats[:, which], rows, core)
        return exchange(out.reshape(rows_n, k_part, tile), "col").sum(axis=0)

    def redistribute(factor, y_first):
        parts = factor.reshape((cols_n, own) + factor.shape[1:]).transpose(0, 2, 1, 3)
        return exchange_permuted(parts, y_first)

    def panel(part, gather):
        return gather(gather_z(part).reshape(-1, tile), "col")

    def owned(both):
        block = pick(both, row, 1)
        block = lax.dynamic_slice_in_dim(block, col * own, own, 2)
        return block.reshape(k_all, own).T

    def joined(parts):
        mine, other = parts
        return jnp.concatenate(
            [jnp.where(core == 0, mine, other), jnp.where(core == 0, other, mine)], axis=-1
        )

    f_one = redistribute(factor_one, True)
    f_two = redistribute(factor_two, False)
    one = solve(heads[0], 0)
    one_mine = panel(one, lax.all_gather)
    one_other = swap(one_mine)
    two = solve(heads[1] - solve(one, 1), 2)
    two_mine = panel(two, share)
    two_other = swap(two_mine)
    remain = vectors[:, 1:, :].transpose(1, 0, 2) - joined([trailing(f_one, p) for p in (one_mine, one_other)])
    remain, two_mine = lax.optimization_barrier((remain, two_mine))
    remaining = remain[1:] - joined([trailing(f_two, p) for p in (two_mine, two_other)])
    first = owned(by_core(core, [one_mine, one_other], 0))
    second = owned(by_core(core, [two_mine, two_other], 0))

    solved = jnp.concatenate([first[None], second[None], remaining]).transpose(1, 0, 2)
    weighted = solved * lumped_mass[:, :, None]
    gram = jnp.einsum("jtk,jtl->kl", weighted, solved, precision=HIGHEST, preferred_element_type=jnp.float32)

    blocks = jnp.stack(
        [gram[i * BLOCK : (i + 1) * BLOCK, j * BLOCK : (j + 1) * BLOCK] for i, j in block_pairs(k_all)]
    )
    blocks = blocks.reshape((2, -1, BLOCK))
    part = pick(blocks, core) + swap(pick(blocks, 1 - core))
    part = exchange(part.reshape(cols_n, -1, BLOCK), "col").sum(axis=0)
    step = 2
    while step < rows_n:
        part = part + sent(part, "row", lambda i: i ^ step)
        step *= 2
    mine = share(part, "col").reshape(-1, BLOCK, BLOCK)
    other = swap(mine)

    inverse = inverse_factor(core, mine, other, k_all, 1.0 / ORDER)
    rotated = jnp.einsum("jtk,lk->jtl", solved, inverse, precision=HIGHEST, preferred_element_type=jnp.float32)
    return (solved, rotated)


def solution(mesh):
    placed = (
        P(("row", "col"), None, None),
        P("row", None, "col"),
        P("row", None, "col"),
        P(None, "row", "col"),
        P(("row", "col"), None),
    )
    return jax.shard_map(
        body,
        mesh=mesh,
        in_specs=placed,
        out_specs=(P(("row", "col"), None, None), P(("row", "col"), None, None)),
        check_vma=False,
    )
```

```python
import functools
import jax
import jax.numpy as jnp
from jax import lax
from jax.experimental import pallas as pl
from jax.experimental.pallas import tpu as pltpu
from jax.sharding import PartitionSpec as P

ORDER = 98304
HIGHEST = lax.Precision.HIGHEST


PIVOTS = 8
BLOCK = 128


def small_dot(a, b, a_dim, b_dim):
    return lax.dot_general(
        a, b, (((a_dim,), (b_dim,)), ((), ())), precision=HIGHEST, preferred_element_type=jnp.float32
    )


def identity(n):
    rows = lax.broadcasted_iota(jnp.int32, (n, n), 0)
    return jnp.where(rows == lax.broadcasted_iota(jnp.int32, (n, n), 1), 1.0, 0.0)


def invert_block(a_ref, b_ref):
    n = a_ref.shape[0]
    full = (PIVOTS, n)
    for lo in range(0, n, PIVOTS):
        block = a_ref[lo : lo + PIVOTS, :]
        other = b_ref[lo : lo + PIVOTS, :]
        d = {
            (i, j): jnp.broadcast_to(block[i : i + 1, lo + j : lo + j + 1], full)
            for i in range(PIVOTS)
            for j in range(i + 1)
        }
        a = [jnp.broadcast_to(block[j : j + 1, :], full) for j in range(PIVOTS)]
        b = [jnp.broadcast_to(other[j : j + 1, :], full) for j in range(PIVOTS)]
        r = {}
        for j in range(PIVOTS):
            r[j] = lax.rsqrt(d[j, j])
            for i in range(j + 1, PIVOTS):
                d[i, j] = d[i, j] * r[j]
            for i in range(j + 1, PIVOTS):
                for k in range(i, PIVOTS):
                    d[k, i] = d[k, i] - d[k, j] * d[i, j]
            a[j] = a[j] * r[j]
            b[j] = b[j] * r[j]
            for i in range(j + 1, PIVOTS):
                a[i] = a[i] - d[i, j] * a[j]
                b[i] = b[i] - d[i, j] * b[j]
        sub = lax.broadcasted_iota(jnp.int32, full, 0)
        done = b[0]
        for j in range(1, PIVOTS):
            done = jnp.where(sub == j, b[j], done)
        b_ref[lo : lo + PIVOTS, :] = done
        for at in range(lo + PIVOTS, n, PIVOTS):
            ah = a_ref[at : at + PIVOTS, :]
            bh = b_ref[at : at + PIVOTS, :]
            c = [jnp.broadcast_to(ah[:, lo + j : lo + j + 1], full) for j in range(PIVOTS)]
            for j in range(PIVOTS):
                c[j] = c[j] * r[j]
                for i in range(j + 1, PIVOTS):
                    c[i] = c[i] - d[i, j] * c[j]
                ah = ah - c[j] * a[j]
                bh = bh - c[j] * b[j]
            a_ref[at : at + PIVOTS, :] = ah
            b_ref[at : at + PIVOTS, :] = bh


def block_pairs(n):
    return [(i, j) for i in range(n // BLOCK) for j in range(i, n // BLOCK)]


def inverse_kernel(scale, core_ref, mine_ref, other_ref, out_ref, a_ref, s_ref, t_ref):
    n = out_ref.shape[0]
    pairs = block_pairs(n)
    half = len(pairs) // 2
    core = core_ref[0]
    for side in range(2):
        for at, (i, j) in enumerate(pairs[side * half : (side + 1) * half]):
            rows, cols = slice(i * BLOCK, (i + 1) * BLOCK), slice(j * BLOCK, (j + 1) * BLOCK)
            part = jnp.where(core == side, mine_ref[at], other_ref[at])
            a_ref[rows, cols] = part * scale
    out_ref[...] = identity(n)

    def one(b, _):
        at = pl.multiple_of(b * BLOCK, BLOCK)
        rows = pl.ds(at, BLOCK)
        s_ref[...] = a_ref[rows, rows]
        t_ref[...] = identity(BLOCK)
        invert_block(s_ref, t_ref)
        inv = t_ref[...]
        below = lax.broadcasted_iota(jnp.int32, (BLOCK, n), 1) >= at + BLOCK
        u = small_dot(inv, jnp.where(below, a_ref[rows, :], 0.0), 1, 0)
        x = small_dot(inv, out_ref[rows, :], 1, 0)
        out_ref[rows, :] = x

        def rest(i, _):
            later = pl.ds(pl.multiple_of(i * BLOCK, BLOCK), BLOCK)
            ui = small_dot(inv, a_ref[rows, later], 1, 0)
            a_ref[later, :] = a_ref[later, :] - small_dot(ui, u, 0, 0)
            out_ref[later, :] = out_ref[later, :] - small_dot(ui, x, 0, 0)
            return 0

        lax.fori_loop(b + 1, n // BLOCK, rest, 0)
        return 0

    lax.fori_loop(0, n // BLOCK, one, 0)


def inverse_factor(core, mine, other, n, scale):
    return pl.pallas_call(
        functools.partial(inverse_kernel, scale),
        out_shape=jax.ShapeDtypeStruct((n, n), jnp.float32),
        in_specs=[pl.BlockSpec(memory_space=pltpu.SMEM)] + [pl.BlockSpec(memory_space=pltpu.VMEM)] * 2,
        out_specs=pl.BlockSpec(memory_space=pltpu.VMEM),
        scratch_shapes=[
            pltpu.VMEM((n, n), jnp.float32),
            pltpu.VMEM((BLOCK, BLOCK), jnp.float32),
            pltpu.VMEM((BLOCK, BLOCK), jnp.float32),
        ],
        compiler_params=pltpu.CompilerParams(vmem_limit_bytes=16 * 1024 * 1024),
    )(jnp.full((1,), core, jnp.int32), mine, other)


def pack_kernel(one_ref, two_ref, out_ref):
    for which, ref in enumerate((one_ref, two_ref)):
        lead = which + 1
        out_ref[0, which, :lead] = jnp.zeros((lead,) + ref.shape[1:], jnp.float32)
        out_ref[0, which, lead:] = ref[...]


def pack(one, two, own):
    rows, steps, tile = one.shape
    blocks = rows // own
    specs = [pl.BlockSpec((f.shape[1], own, tile), lambda c: (0, c, 0)) for f in (one, two)]
    shape = (blocks, 2, steps + 1, own, tile)
    return pl.pallas_call(
        pack_kernel,
        out_shape=jax.ShapeDtypeStruct(shape, jnp.float32),
        grid=(blocks,),
        in_specs=specs,
        out_specs=pl.BlockSpec((1,) + shape[1:], lambda c: (c, 0, 0, 0, 0)),
        compiler_params=pltpu.CompilerParams(vmem_limit_bytes=56 * 1024 * 1024),
        cost_estimate=pl.CostEstimate(flops=0, bytes_accessed=16 * one.size, transcendentals=0),
    )(one.transpose(1, 0, 2), two.transpose(1, 0, 2))


def pair(ref, first, second, rows):
    return jnp.concatenate([ref[first].reshape(rows, BLOCK), ref[second].reshape(rows, BLOCK)], axis=1)


def update_kernel(parity_ref, start_ref, factor_ref, panel_ref, after_ref, out_ref):
    @pl.when(pl.program_id(0) == 0)
    def _():
        out_ref[...] = start_ref[...]

    rows, cols = out_ref.shape
    f = pair(factor_ref, (0, 0, 0), (1, 0, 0), rows)
    p = pair(panel_ref, (slice(None), 0, 0), (slice(None), 1, 0), cols)
    out_ref[...] -= small_dot(f, p, 1, 1)


def update(start, factors, panel, parity, which, after):
    chips = factors.shape[0]
    last = panel.shape[2] - 1
    return pl.pallas_call(
        update_kernel,
        out_shape=jax.ShapeDtypeStruct(start.shape, jnp.float32),
        grid_spec=pltpu.PrefetchScalarGridSpec(
            num_scalar_prefetch=1,
            grid=(chips // 2,),
            in_specs=[
                pl.BlockSpec(start.shape, lambda s, p: (0, 0)),
                pl.BlockSpec((2, 1, 1) + factors.shape[3:], lambda s, p: (s, p[0], which, 0, 0, 0)),
                pl.BlockSpec((panel.shape[0], 2, 1) + panel.shape[3:], lambda s, p: (0, s, p[0] * last, 0, 0)),
                pl.BlockSpec(memory_space=pl.ANY),
            ],
            out_specs=pl.BlockSpec(start.shape, lambda s, p: (0, 0)),
        ),
        compiler_params=pltpu.CompilerParams(vmem_limit_bytes=56 * 1024 * 1024),
        cost_estimate=pl.CostEstimate(
            flops=12 * start.size * chips * BLOCK, bytes_accessed=8 * start.size + 8 * start.size, transcendentals=0
        ),
    )(jnp.full((1,), parity, jnp.int32), start, factors, panel, after)


def finish_kernel(at_ref, update_ref, one_ref, two_ref, mass_ref, solved_ref, blocks_ref):
    rounds, own, k_all = solved_ref.shape
    lanes = lax.broadcasted_iota(jnp.int32, (own, BLOCK), 1)
    rows = lax.broadcasted_iota(jnp.int32, (own, BLOCK), 0)
    take = jnp.where(lanes == rows + at_ref[1] * own, 1.0, 0.0)
    solved_ref[0] = small_dot(take, one_ref[:, 0].reshape(k_all, BLOCK), 1, 1)
    solved_ref[1] = small_dot(take, two_ref[:, 0].reshape(k_all, BLOCK), 1, 1)
    solved_ref[2:] = update_ref[2 * own :, :].reshape(rounds - 2, own, k_all)
    all_rows = solved_ref[...].reshape(own * rounds, k_all)
    weighted = all_rows * mass_ref[...]
    at = 0
    for i in range(k_all // BLOCK):
        got = small_dot(weighted[:, i * BLOCK : (i + 1) * BLOCK], all_rows[:, i * BLOCK :], 0, 0)
        for j in range(k_all // BLOCK - i):
            blocks_ref[at] = got[:, j * BLOCK : (j + 1) * BLOCK]
            at += 1


def finish(updated, one, two, mass, row, col, shape):
    rounds, own, k_all = shape
    count = len(block_pairs(k_all))
    panel = (one.shape[0], 1) + one.shape[2:]
    return pl.pallas_call(
        finish_kernel,
        out_shape=(
            jax.ShapeDtypeStruct(shape, jnp.float32),
            jax.ShapeDtypeStruct((count, BLOCK, BLOCK), jnp.float32),
        ),
        grid_spec=pltpu.PrefetchScalarGridSpec(
            num_scalar_prefetch=1,
            grid=(1,),
            in_specs=[
                pl.BlockSpec(updated.shape, lambda s, at: (0, 0)),
                pl.BlockSpec(panel, lambda s, at: (0, at[0], 0, 0)),
                pl.BlockSpec(panel, lambda s, at: (0, at[0] // 2, 0, 0)),
                pl.BlockSpec((own * rounds, 1), lambda s, at: (0, 0)),
            ],
            out_specs=(
                pl.BlockSpec(shape, lambda s, at: (0, 0, 0)),
                pl.BlockSpec((count, BLOCK, BLOCK), lambda s, at: (0, 0, 0)),
            ),
        ),
        compiler_params=pltpu.CompilerParams(vmem_limit_bytes=24 * 1024 * 1024),
        cost_estimate=pl.CostEstimate(flops=8 * updated.size * k_all, bytes_accessed=12 * updated.size, transcendentals=0),
    )(jnp.stack([row, col]).astype(jnp.int32), updated, one, two, mass.T.reshape(-1, 1))


def exchange(blocks, axis):
    return lax.all_to_all(blocks, axis, 0, 0)


def share(block, axis):
    size = lax.axis_size(axis)
    return exchange(jnp.broadcast_to(block[None], (size,) + block.shape), axis)


def product(rows, tiles):
    return jnp.einsum("rkq,riq->ki", rows, tiles, precision=HIGHEST, preferred_element_type=jnp.float32)


def body(vectors, factor_one, factor_two, block_inverse, lumped_mass):
    rows_n, cols_n = lax.axis_size("row"), lax.axis_size("col")
    row, col = lax.axis_index("row"), lax.axis_index("col")
    core = row % 2
    own, rounds, k_all = vectors.shape
    tile = own * cols_n
    k_part = k_all // cols_n
    swap = [(i, i ^ 1) for i in range(rows_n)]

    mats = jnp.stack([block_inverse[0], factor_one[:, 0, :], block_inverse[1]])
    heads = vectors[:, :2, :].reshape(own, 2, cols_n, k_part).transpose(2, 1, 0, 3)
    mats, heads, factor_one = lax.optimization_barrier((mats, heads, factor_one))
    heads = exchange(heads, "col")
    heads = heads.transpose(1, 3, 0, 2).reshape(2, k_part, tile)
    head_rows = share(heads[0], "row")

    mats = lax.all_gather(mats, "col")

    def half(panel_rows):
        return lax.dynamic_index_in_dim(
            panel_rows.reshape((rows_n // 2, 2) + panel_rows.shape[1:]), core, 1, keepdims=False
        )

    factors = pack(factor_one, factor_two, own)
    factors = exchange(factors, "col")
    mats, factors = lax.optimization_barrier((mats, factors))
    factors = factors.reshape((rows_n // 2, 2) + factors.shape[1:])

    one_rows = share(product(head_rows, mats[:, 0]), "row")
    one_whole = lax.all_gather(one_rows, "col")
    remain_head = heads[1] - product(one_rows, mats[:, 1])
    remain_rows = share(remain_head, "row")
    two_rows = share(product(remain_rows, mats[:, 2]), "row")
    two_mine = share(half(two_rows), "col")

    by_parity = one_whole.reshape((cols_n, rows_n // 2, 2) + one_whole.shape[2:])
    done = vectors.transpose(1, 0, 2).reshape(-1, k_all)
    for parity in (0, 1):
        done = update(done, factors, by_parity, parity, 0, two_rows)
    two_other = lax.ppermute(two_mine, "row", swap)
    done = update(done, factors, two_mine[:, :, None], core, 1, two_rows)
    done = update(done, factors, two_other[:, :, None], 1 - core, 1, two_rows)
    solved, blocks = finish(done, one_whole, two_mine, lumped_mass, row, col, (rounds, own, k_all))
    solved = solved.transpose(1, 0, 2)

    blocks = blocks.reshape((2, -1, BLOCK))
    there = lax.ppermute(lax.dynamic_index_in_dim(blocks, 1 - core, 0, keepdims=False), "row", swap)
    part = lax.dynamic_index_in_dim(blocks, core, 0, keepdims=False) + there
    part = exchange(part.reshape(cols_n, -1, BLOCK), "col").sum(axis=0)
    step = 2
    while step < rows_n:
        part = part + lax.ppermute(part, "row", [(i, i ^ step) for i in range(rows_n)])
        step *= 2
    mine = share(part, "col").reshape(-1, BLOCK, BLOCK)
    other = lax.ppermute(mine, "row", swap)

    inverse = inverse_factor(core, mine, other, k_all, 1.0 / ORDER)
    rotated = jnp.einsum("jtk,lk->jtl", solved, inverse, precision=HIGHEST, preferred_element_type=jnp.float32)
    return (solved, rotated)


def solution(mesh):
    placed = (
        P(("row", "col"), None, None),
        P("row", None, "col"),
        P("row", None, "col"),
        P(None, "row", "col"),
        P(("row", "col"), None),
    )
    return jax.shard_map(
        body,
        mesh=mesh,
        in_specs=placed,
        out_specs=(P(("row", "col"), None, None), P(("row", "col"), None, None)),
        check_vma=False,
    )
```

```python
import functools
import jax
import jax.numpy as jnp
from jax import lax
from jax.experimental import pallas as pl
from jax.experimental.pallas import tpu as pltpu
from jax.sharding import PartitionSpec as P

ORDER = 98304
HIGHEST = lax.Precision.HIGHEST


PIVOTS = 8
BLOCK = 128


def small_dot(a, b, a_dim, b_dim):
    return lax.dot_general(
        a, b, (((a_dim,), (b_dim,)), ((), ())), precision=HIGHEST, preferred_element_type=jnp.float32
    )


def identity(n):
    rows = lax.broadcasted_iota(jnp.int32, (n, n), 0)
    return jnp.where(rows == lax.broadcasted_iota(jnp.int32, (n, n), 1), 1.0, 0.0)


def invert_block(a_ref, b_ref):
    n = a_ref.shape[0]
    full = (PIVOTS, n)
    for lo in range(0, n, PIVOTS):
        block = a_ref[lo : lo + PIVOTS, :]
        other = b_ref[lo : lo + PIVOTS, :]
        d = {
            (i, j): jnp.broadcast_to(block[i : i + 1, lo + j : lo + j + 1], full)
            for i in range(PIVOTS)
            for j in range(i + 1)
        }
        a = [jnp.broadcast_to(block[j : j + 1, :], full) for j in range(PIVOTS)]
        b = [jnp.broadcast_to(other[j : j + 1, :], full) for j in range(PIVOTS)]
        r = {}
        for j in range(PIVOTS):
            r[j] = lax.rsqrt(d[j, j])
            for i in range(j + 1, PIVOTS):
                d[i, j] = d[i, j] * r[j]
            for i in range(j + 1, PIVOTS):
                for k in range(i, PIVOTS):
                    d[k, i] = d[k, i] - d[k, j] * d[i, j]
            a[j] = a[j] * r[j]
            b[j] = b[j] * r[j]
            for i in range(j + 1, PIVOTS):
                a[i] = a[i] - d[i, j] * a[j]
                b[i] = b[i] - d[i, j] * b[j]
        sub = lax.broadcasted_iota(jnp.int32, full, 0)
        done = b[0]
        for j in range(1, PIVOTS):
            done = jnp.where(sub == j, b[j], done)
        b_ref[lo : lo + PIVOTS, :] = done
        for at in range(lo + PIVOTS, n, PIVOTS):
            ah = a_ref[at : at + PIVOTS, :]
            bh = b_ref[at : at + PIVOTS, :]
            c = [jnp.broadcast_to(ah[:, lo + j : lo + j + 1], full) for j in range(PIVOTS)]
            for j in range(PIVOTS):
                c[j] = c[j] * r[j]
                for i in range(j + 1, PIVOTS):
                    c[i] = c[i] - d[i, j] * c[j]
                ah = ah - c[j] * a[j]
                bh = bh - c[j] * b[j]
            a_ref[at : at + PIVOTS, :] = ah
            b_ref[at : at + PIVOTS, :] = bh


def block_pairs(n):
    return [(i, j) for i in range(n // BLOCK) for j in range(i, n // BLOCK)]


def inverse_kernel(scale, core_ref, mine_ref, other_ref, out_ref, a_ref, s_ref, t_ref):
    n = out_ref.shape[0]
    pairs = block_pairs(n)
    half = len(pairs) // 2
    core = core_ref[0]
    for side in range(2):
        for at, (i, j) in enumerate(pairs[side * half : (side + 1) * half]):
            rows, cols = slice(i * BLOCK, (i + 1) * BLOCK), slice(j * BLOCK, (j + 1) * BLOCK)
            part = jnp.where(core == side, mine_ref[at], other_ref[at])
            a_ref[rows, cols] = part * scale
    out_ref[...] = identity(n)

    def one(b, _):
        at = pl.multiple_of(b * BLOCK, BLOCK)
        rows = pl.ds(at, BLOCK)
        s_ref[...] = a_ref[rows, rows]
        t_ref[...] = identity(BLOCK)
        invert_block(s_ref, t_ref)
        inv = t_ref[...]
        below = lax.broadcasted_iota(jnp.int32, (BLOCK, n), 1) >= at + BLOCK
        u = small_dot(inv, jnp.where(below, a_ref[rows, :], 0.0), 1, 0)
        x = small_dot(inv, out_ref[rows, :], 1, 0)
        out_ref[rows, :] = x

        def rest(i, _):
            later = pl.ds(pl.multiple_of(i * BLOCK, BLOCK), BLOCK)
            ui = small_dot(inv, a_ref[rows, later], 1, 0)
            a_ref[later, :] = a_ref[later, :] - small_dot(ui, u, 0, 0)
            out_ref[later, :] = out_ref[later, :] - small_dot(ui, x, 0, 0)
            return 0

        lax.fori_loop(b + 1, n // BLOCK, rest, 0)
        return 0

    lax.fori_loop(0, n // BLOCK, one, 0)


def inverse_factor(core, mine, other, n, scale):
    return pl.pallas_call(
        functools.partial(inverse_kernel, scale),
        out_shape=jax.ShapeDtypeStruct((n, n), jnp.float32),
        in_specs=[pl.BlockSpec(memory_space=pltpu.SMEM)] + [pl.BlockSpec(memory_space=pltpu.VMEM)] * 2,
        out_specs=pl.BlockSpec(memory_space=pltpu.VMEM),
        scratch_shapes=[
            pltpu.VMEM((n, n), jnp.float32),
            pltpu.VMEM((BLOCK, BLOCK), jnp.float32),
            pltpu.VMEM((BLOCK, BLOCK), jnp.float32),
        ],
        compiler_params=pltpu.CompilerParams(vmem_limit_bytes=16 * 1024 * 1024),
    )(jnp.full((1,), core, jnp.int32), mine, other)


def pair(ref, first, second, rows):
    return jnp.concatenate([ref[first].reshape(rows, BLOCK), ref[second].reshape(rows, BLOCK)], axis=1)


def update_kernel(parity_ref, start_ref, factor_ref, panel_ref, out_ref):
    @pl.when(pl.program_id(0) == 0)
    def _():
        out_ref[...] = start_ref[...]

    steps, own = factor_ref.shape[2:4]
    cols = out_ref.shape[1]
    lead = out_ref.shape[0] - steps * own
    f = pair(factor_ref, (0, 0), (1, 0), steps * own)
    p = pair(panel_ref, (slice(None), 0, 0), (slice(None), 0, 1), cols)
    out_ref[lead:, :] -= small_dot(f, p, 1, 1)


def update(start, factor, panels, which, parity):
    chips = factor.shape[0]
    return pl.pallas_call(
        update_kernel,
        out_shape=jax.ShapeDtypeStruct(start.shape, jnp.float32),
        grid_spec=pltpu.PrefetchScalarGridSpec(
            num_scalar_prefetch=1,
            grid=(chips // 2,),
            in_specs=[
                pl.BlockSpec(start.shape, lambda s, p: (0, 0)),
                pl.BlockSpec((2, 1) + factor.shape[2:], lambda s, p: (s, p[0], 0, 0, 0)),
                pl.BlockSpec((panels.shape[0], 1, 2) + panels.shape[3:], lambda s, p: (0, which, s, 0, 0)),
            ],
            out_specs=pl.BlockSpec(start.shape, lambda s, p: (0, 0)),
        ),
        compiler_params=pltpu.CompilerParams(vmem_limit_bytes=56 * 1024 * 1024),
        cost_estimate=pl.CostEstimate(
            flops=12 * start.size * chips * BLOCK, bytes_accessed=8 * start.size + 8 * start.size, transcendentals=0
        ),
    )(jnp.full((1,), parity, jnp.int32), start, factor, panels)


def finish_kernel(at_ref, update_ref, panels_ref, mass_ref, solved_ref, blocks_ref):
    rounds, own, k_all = solved_ref.shape
    lanes = lax.broadcasted_iota(jnp.int32, (own, BLOCK), 1)
    rows = lax.broadcasted_iota(jnp.int32, (own, BLOCK), 0)
    take = jnp.where(lanes == rows + at_ref[1] * own, 1.0, 0.0)
    for which in range(2):
        solved_ref[which] = small_dot(take, panels_ref[:, which, 0].reshape(k_all, BLOCK), 1, 1)
    solved_ref[2:] = update_ref[2 * own :, :].reshape(rounds - 2, own, k_all)
    all_rows = solved_ref[...].reshape(own * rounds, k_all)
    weighted = all_rows * mass_ref[...]
    at = 0
    for i in range(k_all // BLOCK):
        got = small_dot(weighted[:, i * BLOCK : (i + 1) * BLOCK], all_rows[:, i * BLOCK :], 0, 0)
        for j in range(k_all // BLOCK - i):
            blocks_ref[at] = got[:, j * BLOCK : (j + 1) * BLOCK]
            at += 1


def finish(updated, panels, mass, place, col, shape):
    rounds, own, k_all = shape
    count = len(block_pairs(k_all))
    return pl.pallas_call(
        finish_kernel,
        out_shape=(
            jax.ShapeDtypeStruct(shape, jnp.float32),
            jax.ShapeDtypeStruct((count, BLOCK, BLOCK), jnp.float32),
        ),
        grid_spec=pltpu.PrefetchScalarGridSpec(
            num_scalar_prefetch=1,
            grid=(1,),
            in_specs=[
                pl.BlockSpec(updated.shape, lambda s, at: (0, 0)),
                pl.BlockSpec(panels.shape[:2] + (1,) + panels.shape[3:], lambda s, at: (0, 0, at[0], 0, 0)),
                pl.BlockSpec((own * rounds, 1), lambda s, at: (0, 0)),
            ],
            out_specs=(
                pl.BlockSpec(shape, lambda s, at: (0, 0, 0)),
                pl.BlockSpec((count, BLOCK, BLOCK), lambda s, at: (0, 0, 0)),
            ),
        ),
        compiler_params=pltpu.CompilerParams(vmem_limit_bytes=56 * 1024 * 1024),
        cost_estimate=pl.CostEstimate(flops=8 * updated.size * k_all, bytes_accessed=12 * updated.size, transcendentals=0),
    )(jnp.stack([place, col]).astype(jnp.int32), updated, panels, mass.T.reshape(-1, 1))


def exchange(blocks, axis):
    return lax.all_to_all(blocks, axis, 0, 0)


def share(block, axis):
    size = lax.axis_size(axis)
    return exchange(jnp.broadcast_to(block[None], (size,) + block.shape), axis)


def product(rows, tiles):
    return jnp.einsum("rkq,riq->ki", rows, tiles, precision=HIGHEST, preferred_element_type=jnp.float32)


def body(vectors, factor_one, factor_two, block_inverse, lumped_mass):
    rows_n, cols_n = lax.axis_size("row"), lax.axis_size("col")
    row, col = lax.axis_index("row"), lax.axis_index("col")
    core = row % 2
    own, rounds, k_all = vectors.shape
    tile = own * cols_n
    k_part = k_all // cols_n
    swap = [(i, i ^ 1) for i in range(rows_n)]
    turn = [(r * cols_n + c, c * cols_n + r) for r in range(rows_n) for c in range(cols_n)]

    mats = jnp.stack([factor_one[:, 0, :], block_inverse[1]])
    mats = lax.all_gather(mats, "col")

    turned = lax.ppermute(vectors[:, 0, :], ("row", "col"), turn)
    block = share(turned, "row").reshape(tile, k_all)
    parts = jnp.einsum("qk,iq->ki", block, block_inverse[0], precision=HIGHEST, preferred_element_type=jnp.float32)
    one = exchange(parts.reshape(cols_n, k_part, tile), "col").sum(axis=0)

    head = vectors[:, 1, :].reshape(own, cols_n, k_part).transpose(1, 0, 2)
    head = exchange(head, "col")
    head = head.transpose(2, 0, 1).reshape(k_part, tile)

    def half(panel_rows):
        return lax.dynamic_index_in_dim(
            panel_rows.reshape((rows_n // 2, 2) + panel_rows.shape[1:]), core, 1, keepdims=False
        )

    def redistribute(factor):
        parts = factor.reshape((cols_n, own) + factor.shape[1:]).transpose(0, 2, 1, 3)
        parts = exchange(parts, "col")
        return parts.reshape((rows_n // 2, 2) + parts.shape[1:])

    one_rows = share(one, "row")
    remain_head = head - product(one_rows, mats[:, 0])
    remain_rows = share(remain_head, "row")
    two_rows = share(product(remain_rows, mats[:, 1]), "row")
    mine = lax.all_gather(jnp.stack([half(one_rows), half(two_rows)]), "col")
    other = lax.ppermute(mine, "row", swap)
    f_one, f_two = redistribute(factor_one), redistribute(factor_two)

    done = vectors.transpose(1, 0, 2).reshape(-1, k_all)
    for which, factor in enumerate((f_one, f_two)):
        done = update(done, factor, mine, which, core)
        done = update(done, factor, other, which, 1 - core)
    solved, blocks = finish(done, mine, lumped_mass, row // 2, col, (rounds, own, k_all))
    solved = solved.transpose(1, 0, 2)

    blocks = blocks.reshape((2, -1, BLOCK))
    there = lax.ppermute(lax.dynamic_index_in_dim(blocks, 1 - core, 0, keepdims=False), "row", swap)
    part = lax.dynamic_index_in_dim(blocks, core, 0, keepdims=False) + there
    part = exchange(part.reshape(cols_n, -1, BLOCK), "col").sum(axis=0)
    step = 2
    while step < rows_n:
        part = part + lax.ppermute(part, "row", [(i, i ^ step) for i in range(rows_n)])
        step *= 2
    mine = share(part, "col").reshape(-1, BLOCK, BLOCK)
    other = lax.ppermute(mine, "row", swap)

    inverse = inverse_factor(core, mine, other, k_all, 1.0 / ORDER)
    rotated = jnp.einsum("jtk,lk->jtl", solved, inverse, precision=HIGHEST, preferred_element_type=jnp.float32)
    return (solved, rotated)


def solution(mesh):
    placed = (
        P(("row", "col"), None, None),
        P("row", None, "col"),
        P("row", None, "col"),
        P(None, "row", "col"),
        P(("row", "col"), None),
    )
    return jax.shard_map(
        body,
        mesh=mesh,
        in_specs=placed,
        out_specs=(P(("row", "col"), None, None), P(("row", "col"), None, None)),
        check_vma=False,
    )
```

```python
import functools
import jax
import jax.numpy as jnp
from jax import lax
from jax.experimental import pallas as pl
from jax.experimental.pallas import tpu as pltpu
from jax.sharding import PartitionSpec as P

ORDER = 98304
HIGHEST = lax.Precision.HIGHEST


PIVOTS = 8
BLOCK = 128


def small_dot(a, b, a_dim, b_dim):
    return lax.dot_general(
        a, b, (((a_dim,), (b_dim,)), ((), ())), precision=HIGHEST, preferred_element_type=jnp.float32
    )


def identity(n):
    rows = lax.broadcasted_iota(jnp.int32, (n, n), 0)
    return jnp.where(rows == lax.broadcasted_iota(jnp.int32, (n, n), 1), 1.0, 0.0)


def invert_block(a_ref, b_ref):
    n = a_ref.shape[0]
    full = (PIVOTS, n)
    for lo in range(0, n, PIVOTS):
        block = a_ref[lo : lo + PIVOTS, :]
        other = b_ref[lo : lo + PIVOTS, :]
        d = {
            (i, j): jnp.broadcast_to(block[i : i + 1, lo + j : lo + j + 1], full)
            for i in range(PIVOTS)
            for j in range(i + 1)
        }
        a = [jnp.broadcast_to(block[j : j + 1, :], full) for j in range(PIVOTS)]
        b = [jnp.broadcast_to(other[j : j + 1, :], full) for j in range(PIVOTS)]
        r = {}
        for j in range(PIVOTS):
            r[j] = lax.rsqrt(d[j, j])
            for i in range(j + 1, PIVOTS):
                d[i, j] = d[i, j] * r[j]
            for i in range(j + 1, PIVOTS):
                for k in range(i, PIVOTS):
                    d[k, i] = d[k, i] - d[k, j] * d[i, j]
            a[j] = a[j] * r[j]
            b[j] = b[j] * r[j]
            for i in range(j + 1, PIVOTS):
                a[i] = a[i] - d[i, j] * a[j]
                b[i] = b[i] - d[i, j] * b[j]
        sub = lax.broadcasted_iota(jnp.int32, full, 0)
        done = b[0]
        for j in range(1, PIVOTS):
            done = jnp.where(sub == j, b[j], done)
        b_ref[lo : lo + PIVOTS, :] = done
        for at in range(lo + PIVOTS, n, PIVOTS):
            ah = a_ref[at : at + PIVOTS, :]
            bh = b_ref[at : at + PIVOTS, :]
            c = [jnp.broadcast_to(ah[:, lo + j : lo + j + 1], full) for j in range(PIVOTS)]
            for j in range(PIVOTS):
                c[j] = c[j] * r[j]
                for i in range(j + 1, PIVOTS):
                    c[i] = c[i] - d[i, j] * c[j]
                ah = ah - c[j] * a[j]
                bh = bh - c[j] * b[j]
            a_ref[at : at + PIVOTS, :] = ah
            b_ref[at : at + PIVOTS, :] = bh


def block_pairs(n):
    return [(i, j) for i in range(n // BLOCK) for j in range(i, n // BLOCK)]


def inverse_kernel(scale, core_ref, mine_ref, other_ref, out_ref, a_ref, s_ref, t_ref):
    n = out_ref.shape[0]
    pairs = block_pairs(n)
    half = len(pairs) // 2
    core = core_ref[0]
    for side in range(2):
        for at, (i, j) in enumerate(pairs[side * half : (side + 1) * half]):
            rows, cols = slice(i * BLOCK, (i + 1) * BLOCK), slice(j * BLOCK, (j + 1) * BLOCK)
            part = jnp.where(core == side, mine_ref[at], other_ref[at])
            a_ref[rows, cols] = part * scale
    out_ref[...] = identity(n)

    def one(b, _):
        at = pl.multiple_of(b * BLOCK, BLOCK)
        rows = pl.ds(at, BLOCK)
        s_ref[...] = a_ref[rows, rows]
        t_ref[...] = identity(BLOCK)
        invert_block(s_ref, t_ref)
        inv = t_ref[...]
        below = lax.broadcasted_iota(jnp.int32, (BLOCK, n), 1) >= at + BLOCK
        u = small_dot(inv, jnp.where(below, a_ref[rows, :], 0.0), 1, 0)
        x = small_dot(inv, out_ref[rows, :], 1, 0)
        out_ref[rows, :] = x

        def rest(i, _):
            later = pl.ds(pl.multiple_of(i * BLOCK, BLOCK), BLOCK)
            ui = small_dot(inv, a_ref[rows, later], 1, 0)
            a_ref[later, :] = a_ref[later, :] - small_dot(ui, u, 0, 0)
            out_ref[later, :] = out_ref[later, :] - small_dot(ui, x, 0, 0)
            return 0

        lax.fori_loop(b + 1, n // BLOCK, rest, 0)
        return 0

    lax.fori_loop(0, n // BLOCK, one, 0)


def inverse_factor(core, mine, other, n, scale):
    return pl.pallas_call(
        functools.partial(inverse_kernel, scale),
        out_shape=jax.ShapeDtypeStruct((n, n), jnp.float32),
        in_specs=[pl.BlockSpec(memory_space=pltpu.SMEM)] + [pl.BlockSpec(memory_space=pltpu.VMEM)] * 2,
        out_specs=pl.BlockSpec(memory_space=pltpu.VMEM),
        scratch_shapes=[
            pltpu.VMEM((n, n), jnp.float32),
            pltpu.VMEM((BLOCK, BLOCK), jnp.float32),
            pltpu.VMEM((BLOCK, BLOCK), jnp.float32),
        ],
        compiler_params=pltpu.CompilerParams(vmem_limit_bytes=16 * 1024 * 1024),
    )(jnp.full((1,), core, jnp.int32), mine, other)


def update_kernel(core_ref, start_ref, factor_ref, mine_ref, other_ref, out_ref):
    @pl.when(pl.program_id(0) == 0)
    def _():
        out_ref[...] = start_ref[...]

    chips, _, steps, own, _ = factor_ref.shape
    cols = out_ref.shape[1]
    lead = out_ref.shape[0] - steps * own
    f, p = [], []
    for ref, parity in ((mine_ref, core_ref[0]), (other_ref, 1 - core_ref[0])):
        for z in range(chips):
            f.append(factor_ref[z, parity].reshape(steps * own, BLOCK))
            p.append(ref[:, 0, z].reshape(cols, BLOCK))
    out_ref[lead:, :] -= small_dot(jnp.concatenate(f, axis=1), jnp.concatenate(p, axis=1), 1, 1)


def update(start, factor, mine, other, which, core):
    chips = factor.shape[0]
    panel = pl.BlockSpec((mine.shape[0], 1, 2) + mine.shape[3:], lambda s, p: (0, which, s, 0, 0))
    return pl.pallas_call(
        update_kernel,
        out_shape=jax.ShapeDtypeStruct(start.shape, jnp.float32),
        grid_spec=pltpu.PrefetchScalarGridSpec(
            num_scalar_prefetch=1,
            grid=(chips // 2,),
            in_specs=[
                pl.BlockSpec(start.shape, lambda s, p: (0, 0)),
                pl.BlockSpec((2,) + factor.shape[1:], lambda s, p: (s, 0, 0, 0, 0)),
                panel,
                panel,
            ],
            out_specs=pl.BlockSpec(start.shape, lambda s, p: (0, 0)),
        ),
        compiler_params=pltpu.CompilerParams(vmem_limit_bytes=56 * 1024 * 1024),
        cost_estimate=pl.CostEstimate(
            flops=24 * start.size * chips * BLOCK, bytes_accessed=24 * start.size, transcendentals=0
        ),
    )(jnp.full((1,), core, jnp.int32), start, factor, mine, other)


def finish_kernel(at_ref, update_ref, panels_ref, mass_ref, solved_ref, blocks_ref):
    rounds, own, k_all = solved_ref.shape
    lanes = lax.broadcasted_iota(jnp.int32, (own, BLOCK), 1)
    rows = lax.broadcasted_iota(jnp.int32, (own, BLOCK), 0)
    take = jnp.where(lanes == rows + at_ref[1] * own, 1.0, 0.0)
    for which in range(2):
        solved_ref[which] = small_dot(take, panels_ref[:, which, 0].reshape(k_all, BLOCK), 1, 1)
    solved_ref[2:] = update_ref[2 * own :, :].reshape(rounds - 2, own, k_all)
    all_rows = solved_ref[...].reshape(own * rounds, k_all)
    weighted = all_rows * mass_ref[...]
    at = 0
    for i in range(k_all // BLOCK):
        got = small_dot(weighted[:, i * BLOCK : (i + 1) * BLOCK], all_rows[:, i * BLOCK :], 0, 0)
        for j in range(k_all // BLOCK - i):
            blocks_ref[at] = got[:, j * BLOCK : (j + 1) * BLOCK]
            at += 1


def finish(updated, panels, mass, place, col, shape):
    rounds, own, k_all = shape
    count = len(block_pairs(k_all))
    return pl.pallas_call(
        finish_kernel,
        out_shape=(
            jax.ShapeDtypeStruct(shape, jnp.float32),
            jax.ShapeDtypeStruct((count, BLOCK, BLOCK), jnp.float32),
        ),
        grid_spec=pltpu.PrefetchScalarGridSpec(
            num_scalar_prefetch=1,
            grid=(1,),
            in_specs=[
                pl.BlockSpec(updated.shape, lambda s, at: (0, 0)),
                pl.BlockSpec(panels.shape[:2] + (1,) + panels.shape[3:], lambda s, at: (0, 0, at[0], 0, 0)),
                pl.BlockSpec((own * rounds, 1), lambda s, at: (0, 0)),
            ],
            out_specs=(
                pl.BlockSpec(shape, lambda s, at: (0, 0, 0)),
                pl.BlockSpec((count, BLOCK, BLOCK), lambda s, at: (0, 0, 0)),
            ),
        ),
        compiler_params=pltpu.CompilerParams(vmem_limit_bytes=56 * 1024 * 1024),
        cost_estimate=pl.CostEstimate(flops=8 * updated.size * k_all, bytes_accessed=12 * updated.size, transcendentals=0),
    )(jnp.stack([place, col]).astype(jnp.int32), updated, panels, mass.T.reshape(-1, 1))


def exchange(blocks, axis):
    return lax.all_to_all(blocks, axis, 0, 0)


def share(block, axis):
    size = lax.axis_size(axis)
    return exchange(jnp.broadcast_to(block[None], (size,) + block.shape), axis)


def gather_row(block):
    size = lax.axis_size("row")
    row = lax.axis_index("row")
    step, axis = size // 2, 0
    while step:
        got = lax.ppermute(block, "row", [(i, i ^ step) for i in range(size)])
        upper = (row & step) != 0
        block = jnp.stack([jnp.where(upper, got, block), jnp.where(upper, block, got)], axis=axis)
        step, axis = step // 2, axis + 1
    return block.reshape((size,) + block.shape[axis:])


def product_kernel(rows_ref, tiles_ref, after_ref, out_ref):
    count = rows_ref.shape[0]
    rows = jnp.concatenate([rows_ref[r] for r in range(count)], axis=1)
    tiles = jnp.concatenate([tiles_ref[r, 0] for r in range(count)], axis=1)
    out_ref[...] = small_dot(rows, tiles, 1, 1)


def product(rows, tiles, which, after):
    shape = (rows.shape[1], tiles.shape[2])
    return pl.pallas_call(
        product_kernel,
        out_shape=jax.ShapeDtypeStruct(shape, jnp.float32),
        grid=(1,),
        in_specs=[
            pl.BlockSpec(rows.shape, lambda s: (0, 0, 0)),
            pl.BlockSpec((tiles.shape[0], 1) + tiles.shape[2:], lambda s: (0, which, 0, 0)),
            pl.BlockSpec(memory_space=pl.ANY),
        ],
        out_specs=pl.BlockSpec(shape, lambda s: (0, 0)),
        compiler_params=pltpu.CompilerParams(vmem_limit_bytes=56 * 1024 * 1024),
        cost_estimate=pl.CostEstimate(
            flops=12 * rows.size * tiles.shape[2], bytes_accessed=4 * (rows.size + tiles.size // 2), transcendentals=0
        ),
    )(rows, tiles, after)


def halves_kernel(core_ref, one_ref, two_ref, after_ref, out_ref):
    out_ref[0] = one_ref[:, 0]
    out_ref[1] = two_ref[:, 0]


def halves(one, two, core, after):
    pairs = (one.shape[0] // 2, 2) + one.shape[1:]
    half = pl.BlockSpec((pairs[0], 1) + pairs[2:], lambda s, p: (0, p[0], 0, 0))
    shape = (2, pairs[0]) + pairs[2:]
    return pl.pallas_call(
        halves_kernel,
        out_shape=jax.ShapeDtypeStruct(shape, jnp.float32),
        grid_spec=pltpu.PrefetchScalarGridSpec(
            num_scalar_prefetch=1,
            grid=(1,),
            in_specs=[half, half, pl.BlockSpec(memory_space=pl.ANY)],
            out_specs=pl.BlockSpec(shape, lambda s, p: (0, 0, 0, 0)),
        ),
        compiler_params=pltpu.CompilerParams(vmem_limit_bytes=56 * 1024 * 1024),
        cost_estimate=pl.CostEstimate(flops=0, bytes_accessed=8 * one.size, transcendentals=0),
    )(jnp.full((1,), core, jnp.int32), one.reshape(pairs), two.reshape(pairs), after)


def body(vectors, factor_one, factor_two, block_inverse, lumped_mass):
    rows_n, cols_n = lax.axis_size("row"), lax.axis_size("col")
    row, col = lax.axis_index("row"), lax.axis_index("col")
    core = row % 2
    own, rounds, k_all = vectors.shape
    tile = own * cols_n
    k_part = k_all // cols_n
    swap = [(i, i ^ 1) for i in range(rows_n)]
    turn = [(r * cols_n + c, c * cols_n + r) for r in range(rows_n) for c in range(cols_n)]

    mats = jnp.stack([factor_one[:, 0, :], block_inverse[1]])
    mats = lax.all_gather(mats, "col")

    turned = lax.ppermute(vectors[:, 0, :], ("row", "col"), turn)
    block = gather_row(turned).reshape(tile, k_all)
    parts = jnp.einsum("qk,iq->ki", block, block_inverse[0], precision=HIGHEST, preferred_element_type=jnp.float32)
    head = vectors[:, 1, :].reshape(own, cols_n, k_part).transpose(1, 0, 2).reshape(cols_n, -1, BLOCK)
    head_rows = head.shape[1]
    head = jnp.pad(head, ((0, 0), (0, own - head_rows), (0, 0)))
    both = exchange(jnp.concatenate([parts.reshape(cols_n, k_part, tile), head], axis=1), "col")
    one = both[:, :k_part].sum(axis=0)
    head = both[:, k_part : k_part + head_rows].reshape(cols_n, own, k_part)
    head = head.transpose(2, 0, 1).reshape(k_part, tile)

    def redistribute(factor):
        parts = factor.reshape((cols_n, own) + factor.shape[1:]).transpose(0, 2, 1, 3)
        parts = exchange(parts, "col")
        return parts.reshape((rows_n // 2, 2) + parts.shape[1:])

    one_rows = gather_row(one)
    f_one = redistribute(factor_one)
    f_two = redistribute(factor_two)
    remain_head = head - product(one_rows, mats, 0, one_rows)
    remain_rows = gather_row(remain_head)
    two_rows = gather_row(product(remain_rows, mats, 1, f_one))
    mine = lax.all_gather(halves(one_rows, two_rows, core, f_two), "col")
    other = lax.ppermute(mine, "row", swap)

    done = vectors.transpose(1, 0, 2).reshape(-1, k_all)
    for which, factor in enumerate((f_one, f_two)):
        done = update(done, factor, mine, other, which, core)
    solved, blocks = finish(done, mine, lumped_mass, row // 2, col, (rounds, own, k_all))
    solved = solved.transpose(1, 0, 2)

    blocks = blocks.reshape((2, -1, BLOCK))
    there = lax.ppermute(lax.dynamic_index_in_dim(blocks, 1 - core, 0, keepdims=False), "row", swap)
    part = lax.dynamic_index_in_dim(blocks, core, 0, keepdims=False) + there
    part = exchange(part.reshape(cols_n, -1, BLOCK), "col").sum(axis=0)
    step = 2
    while step < rows_n:
        part = part + lax.ppermute(part, "row", [(i, i ^ step) for i in range(rows_n)])
        step *= 2
    mine = share(part, "col").reshape(-1, BLOCK, BLOCK)
    other = lax.ppermute(mine, "row", swap)

    inverse = inverse_factor(core, mine, other, k_all, 1.0 / ORDER)
    rotated = jnp.einsum("jtk,lk->jtl", solved, inverse, precision=HIGHEST, preferred_element_type=jnp.float32)
    return (solved, rotated)


def solution(mesh):
    placed = (
        P(("row", "col"), None, None),
        P("row", None, "col"),
        P("row", None, "col"),
        P(None, "row", "col"),
        P(("row", "col"), None),
    )
    return jax.shard_map(
        body,
        mesh=mesh,
        in_specs=placed,
        out_specs=(P(("row", "col"), None, None), P(("row", "col"), None, None)),
        check_vma=False,
    )
```

```python
import functools
import jax
import jax.numpy as jnp
from jax import lax
from jax.experimental import pallas as pl
from jax.experimental.pallas import tpu as pltpu
from jax.sharding import PartitionSpec as P

ORDER = 98304
HIGHEST = lax.Precision.HIGHEST


PIVOTS = 8
BLOCK = 128


def small_dot(a, b, a_dim, b_dim):
    return lax.dot_general(
        a, b, (((a_dim,), (b_dim,)), ((), ())), precision=HIGHEST, preferred_element_type=jnp.float32
    )


def identity(n):
    rows = lax.broadcasted_iota(jnp.int32, (n, n), 0)
    return jnp.where(rows == lax.broadcasted_iota(jnp.int32, (n, n), 1), 1.0, 0.0)


def invert_block(a_ref, b_ref):
    n = a_ref.shape[0]
    full = (PIVOTS, n)
    for lo in range(0, n, PIVOTS):
        block = a_ref[lo : lo + PIVOTS, :]
        other = b_ref[lo : lo + PIVOTS, :]
        d = {
            (i, j): jnp.broadcast_to(block[i : i + 1, lo + j : lo + j + 1], full)
            for i in range(PIVOTS)
            for j in range(i + 1)
        }
        a = [jnp.broadcast_to(block[j : j + 1, :], full) for j in range(PIVOTS)]
        b = [jnp.broadcast_to(other[j : j + 1, :], full) for j in range(PIVOTS)]
        r = {}
        for j in range(PIVOTS):
            r[j] = lax.rsqrt(d[j, j])
            for i in range(j + 1, PIVOTS):
                d[i, j] = d[i, j] * r[j]
            for i in range(j + 1, PIVOTS):
                for k in range(i, PIVOTS):
                    d[k, i] = d[k, i] - d[k, j] * d[i, j]
            a[j] = a[j] * r[j]
            b[j] = b[j] * r[j]
            for i in range(j + 1, PIVOTS):
                a[i] = a[i] - d[i, j] * a[j]
                b[i] = b[i] - d[i, j] * b[j]
        sub = lax.broadcasted_iota(jnp.int32, full, 0)
        done = b[0]
        for j in range(1, PIVOTS):
            done = jnp.where(sub == j, b[j], done)
        b_ref[lo : lo + PIVOTS, :] = done
        for at in range(lo + PIVOTS, n, PIVOTS):
            ah = a_ref[at : at + PIVOTS, :]
            bh = b_ref[at : at + PIVOTS, :]
            c = [jnp.broadcast_to(ah[:, lo + j : lo + j + 1], full) for j in range(PIVOTS)]
            for j in range(PIVOTS):
                c[j] = c[j] * r[j]
                for i in range(j + 1, PIVOTS):
                    c[i] = c[i] - d[i, j] * c[j]
                ah = ah - c[j] * a[j]
                bh = bh - c[j] * b[j]
            a_ref[at : at + PIVOTS, :] = ah
            b_ref[at : at + PIVOTS, :] = bh


def block_pairs(n):
    return [(i, j) for i in range(n // BLOCK) for j in range(i, n // BLOCK)]


def inverse_kernel(scale, core_ref, mine_ref, other_ref, out_ref, a_ref, s_ref, t_ref):
    n = out_ref.shape[0]
    pairs = block_pairs(n)
    half = len(pairs) // 2
    core = core_ref[0]
    for side in range(2):
        for at, (i, j) in enumerate(pairs[side * half : (side + 1) * half]):
            rows, cols = slice(i * BLOCK, (i + 1) * BLOCK), slice(j * BLOCK, (j + 1) * BLOCK)
            part = jnp.where(core == side, mine_ref[at], other_ref[at])
            a_ref[rows, cols] = part * scale
    out_ref[...] = identity(n)

    def one(b, _):
        at = pl.multiple_of(b * BLOCK, BLOCK)
        rows = pl.ds(at, BLOCK)
        s_ref[...] = a_ref[rows, rows]
        t_ref[...] = identity(BLOCK)
        invert_block(s_ref, t_ref)
        inv = t_ref[...]
        below = lax.broadcasted_iota(jnp.int32, (BLOCK, n), 1) >= at + BLOCK
        u = small_dot(inv, jnp.where(below, a_ref[rows, :], 0.0), 1, 0)
        x = small_dot(inv, out_ref[rows, :], 1, 0)
        out_ref[rows, :] = x

        def rest(i, _):
            later = pl.ds(pl.multiple_of(i * BLOCK, BLOCK), BLOCK)
            ui = small_dot(inv, a_ref[rows, later], 1, 0)
            a_ref[later, :] = a_ref[later, :] - small_dot(ui, u, 0, 0)
            out_ref[later, :] = out_ref[later, :] - small_dot(ui, x, 0, 0)
            return 0

        lax.fori_loop(b + 1, n // BLOCK, rest, 0)
        return 0

    lax.fori_loop(0, n // BLOCK, one, 0)


def inverse_factor(core, mine, other, n, scale):
    return pl.pallas_call(
        functools.partial(inverse_kernel, scale),
        out_shape=jax.ShapeDtypeStruct((n, n), jnp.float32),
        in_specs=[pl.BlockSpec(memory_space=pltpu.SMEM)] + [pl.BlockSpec(memory_space=pltpu.VMEM)] * 2,
        out_specs=pl.BlockSpec(memory_space=pltpu.VMEM),
        scratch_shapes=[
            pltpu.VMEM((n, n), jnp.float32),
            pltpu.VMEM((BLOCK, BLOCK), jnp.float32),
            pltpu.VMEM((BLOCK, BLOCK), jnp.float32),
        ],
        compiler_params=pltpu.CompilerParams(vmem_limit_bytes=16 * 1024 * 1024),
    )(jnp.full((1,), core, jnp.int32), mine, other)


def update_kernel(core_ref, start_ref, factor_ref, mine_ref, other_ref, out_ref):
    @pl.when(pl.program_id(0) == 0)
    def _():
        out_ref[...] = start_ref[...]

    chips, _, steps, own, _ = factor_ref.shape
    cols = out_ref.shape[1]
    lead = out_ref.shape[0] - steps * own
    f, p = [], []
    for ref, parity in ((mine_ref, core_ref[0]), (other_ref, 1 - core_ref[0])):
        for z in range(chips):
            f.append(factor_ref[z, parity].reshape(steps * own, BLOCK))
            p.append(ref[:, z].reshape(cols, BLOCK))
    out_ref[lead:, :] -= small_dot(jnp.concatenate(f, axis=1), jnp.concatenate(p, axis=1), 1, 1)


def update(start, factor, mine, other, core):
    chips = factor.shape[0]
    panel = pl.BlockSpec((mine.shape[0], 2) + mine.shape[2:], lambda s, p: (0, s, 0, 0))
    return pl.pallas_call(
        update_kernel,
        out_shape=jax.ShapeDtypeStruct(start.shape, jnp.float32),
        grid_spec=pltpu.PrefetchScalarGridSpec(
            num_scalar_prefetch=1,
            grid=(chips // 2,),
            in_specs=[
                pl.BlockSpec(start.shape, lambda s, p: (0, 0)),
                pl.BlockSpec((2,) + factor.shape[1:], lambda s, p: (s, 0, 0, 0, 0)),
                panel,
                panel,
            ],
            out_specs=pl.BlockSpec(start.shape, lambda s, p: (0, 0)),
        ),
        compiler_params=pltpu.CompilerParams(vmem_limit_bytes=56 * 1024 * 1024),
        cost_estimate=pl.CostEstimate(
            flops=24 * start.size * chips * BLOCK, bytes_accessed=24 * start.size, transcendentals=0
        ),
    )(jnp.full((1,), core, jnp.int32), start, factor, mine, other)


def finish_kernel(at_ref, update_ref, one_ref, two_ref, mass_ref, solved_ref, blocks_ref):
    rounds, own, k_all = solved_ref.shape
    lanes = lax.broadcasted_iota(jnp.int32, (own, BLOCK), 1)
    rows = lax.broadcasted_iota(jnp.int32, (own, BLOCK), 0)
    take = jnp.where(lanes == rows + at_ref[1] * own, 1.0, 0.0)
    for which, ref in enumerate((one_ref, two_ref)):
        solved_ref[which] = small_dot(take, ref[:, 0].reshape(k_all, BLOCK), 1, 1)
    solved_ref[2:] = update_ref[2 * own :, :].reshape(rounds - 2, own, k_all)
    all_rows = solved_ref[...].reshape(own * rounds, k_all)
    weighted = all_rows * mass_ref[...]
    at = 0
    for i in range(k_all // BLOCK):
        got = small_dot(weighted[:, i * BLOCK : (i + 1) * BLOCK], all_rows[:, i * BLOCK :], 0, 0)
        for j in range(k_all // BLOCK - i):
            blocks_ref[at] = got[:, j * BLOCK : (j + 1) * BLOCK]
            at += 1


def finish(updated, one, two, mass, place, col, shape):
    rounds, own, k_all = shape
    panel = pl.BlockSpec((one.shape[0], 1) + one.shape[2:], lambda s, at: (0, at[0], 0, 0))
    count = len(block_pairs(k_all))
    return pl.pallas_call(
        finish_kernel,
        out_shape=(
            jax.ShapeDtypeStruct(shape, jnp.float32),
            jax.ShapeDtypeStruct((count, BLOCK, BLOCK), jnp.float32),
        ),
        grid_spec=pltpu.PrefetchScalarGridSpec(
            num_scalar_prefetch=1,
            grid=(1,),
            in_specs=[
                pl.BlockSpec(updated.shape, lambda s, at: (0, 0)),
                panel,
                panel,
                pl.BlockSpec((own * rounds, 1), lambda s, at: (0, 0)),
            ],
            out_specs=(
                pl.BlockSpec(shape, lambda s, at: (0, 0, 0)),
                pl.BlockSpec((count, BLOCK, BLOCK), lambda s, at: (0, 0, 0)),
            ),
        ),
        compiler_params=pltpu.CompilerParams(vmem_limit_bytes=56 * 1024 * 1024),
        cost_estimate=pl.CostEstimate(flops=8 * updated.size * k_all, bytes_accessed=12 * updated.size, transcendentals=0),
    )(jnp.stack([place, col]).astype(jnp.int32), updated, one, two, mass.T.reshape(-1, 1))


def exchange(blocks, axis):
    return lax.all_to_all(blocks, axis, 0, 0)


def share(block, axis):
    size = lax.axis_size(axis)
    return exchange(jnp.broadcast_to(block[None], (size,) + block.shape), axis)


def gather_row(block):
    size = lax.axis_size("row")
    row = lax.axis_index("row")
    step, axis = size // 2, 0
    while step:
        got = lax.ppermute(block, "row", [(i, i ^ step) for i in range(size)])
        upper = (row & step) != 0
        block = jnp.stack([jnp.where(upper, got, block), jnp.where(upper, block, got)], axis=axis)
        step, axis = step // 2, axis + 1
    return block.reshape((size,) + block.shape[axis:])


def product_kernel(rows_ref, tiles_ref, after_ref, out_ref):
    count = rows_ref.shape[0]
    rows = jnp.concatenate([rows_ref[r] for r in range(count)], axis=1)
    tiles = jnp.concatenate([tiles_ref[r, 0] for r in range(count)], axis=1)
    out_ref[...] = small_dot(rows, tiles, 1, 1)


def product(rows, tiles, which, after):
    shape = (rows.shape[1], tiles.shape[2])
    return pl.pallas_call(
        product_kernel,
        out_shape=jax.ShapeDtypeStruct(shape, jnp.float32),
        grid=(1,),
        in_specs=[
            pl.BlockSpec(rows.shape, lambda s: (0, 0, 0)),
            pl.BlockSpec((tiles.shape[0], 1) + tiles.shape[2:], lambda s: (0, which, 0, 0)),
            pl.BlockSpec(memory_space=pl.ANY),
        ],
        out_specs=pl.BlockSpec(shape, lambda s: (0, 0)),
        compiler_params=pltpu.CompilerParams(vmem_limit_bytes=56 * 1024 * 1024),
        cost_estimate=pl.CostEstimate(
            flops=12 * rows.size * tiles.shape[2], bytes_accessed=4 * (rows.size + tiles.size // 2), transcendentals=0
        ),
    )(rows, tiles, after)


def hold_kernel(block_ref, after_ref, out_ref):
    out_ref[...] = block_ref[...]


def hold(block, after):
    return pl.pallas_call(
        hold_kernel,
        out_shape=jax.ShapeDtypeStruct(block.shape, block.dtype),
        in_specs=[pl.BlockSpec(memory_space=pltpu.VMEM), pl.BlockSpec(memory_space=pl.ANY)],
        out_specs=pl.BlockSpec(memory_space=pltpu.VMEM),
        cost_estimate=pl.CostEstimate(flops=0, bytes_accessed=8 * block.size, transcendentals=0),
    )(block, after)


def half_kernel(core_ref, panel_ref, first_ref, second_ref, out_ref):
    out_ref[...] = panel_ref[:, 0]


def half(panel, core, first, second):
    pairs = (panel.shape[0] // 2, 2) + panel.shape[1:]
    shape = (pairs[0],) + pairs[2:]
    after = pl.BlockSpec(memory_space=pl.ANY)
    return pl.pallas_call(
        half_kernel,
        out_shape=jax.ShapeDtypeStruct(shape, jnp.float32),
        grid_spec=pltpu.PrefetchScalarGridSpec(
            num_scalar_prefetch=1,
            grid=(1,),
            in_specs=[pl.BlockSpec((pairs[0], 1) + pairs[2:], lambda s, p: (0, p[0], 0, 0)), after, after],
            out_specs=pl.BlockSpec(shape, lambda s, p: (0, 0, 0)),
        ),
        compiler_params=pltpu.CompilerParams(vmem_limit_bytes=56 * 1024 * 1024),
        cost_estimate=pl.CostEstimate(flops=0, bytes_accessed=4 * panel.size, transcendentals=0),
    )(jnp.full((1,), core, jnp.int32), panel.reshape(pairs), first, second)


def body(vectors, factor_one, factor_two, block_inverse, lumped_mass):
    rows_n, cols_n = lax.axis_size("row"), lax.axis_size("col")
    row, col = lax.axis_index("row"), lax.axis_index("col")
    core = row % 2
    own, rounds, k_all = vectors.shape
    tile = own * cols_n
    k_part = k_all // cols_n
    swap = [(i, i ^ 1) for i in range(rows_n)]
    turn = [(r * cols_n + c, c * cols_n + r) for r in range(rows_n) for c in range(cols_n)]

    stack = jnp.stack([factor_one[:, 0, :], block_inverse[1]])
    mats = lax.all_gather(stack, "col")

    turned = lax.ppermute(hold(vectors[:, 0, :], stack), ("row", "col"), turn)
    block = gather_row(turned).reshape(tile, k_all)
    parts = jnp.einsum("qk,iq->ki", block, block_inverse[0], precision=HIGHEST, preferred_element_type=jnp.float32)
    head = vectors[:, 1, :].reshape(own, cols_n, k_part).transpose(1, 0, 2).reshape(cols_n, -1, BLOCK)
    head_rows = head.shape[1]
    head = jnp.pad(head, ((0, 0), (0, own - head_rows), (0, 0)))
    both = exchange(jnp.concatenate([parts.reshape(cols_n, k_part, tile), head], axis=1), "col")
    one = both[:, :k_part].sum(axis=0)
    head = both[:, k_part : k_part + head_rows].reshape(cols_n, own, k_part)
    head = head.transpose(2, 0, 1).reshape(k_part, tile)

    def redistribute(factor):
        parts = factor.reshape((cols_n, own) + factor.shape[1:]).transpose(0, 2, 1, 3)
        parts = exchange(parts, "col")
        return parts.reshape((rows_n // 2, 2) + parts.shape[1:])

    one_rows = gather_row(one)
    f_one = redistribute(factor_one)
    f_two = redistribute(factor_two)
    remain_head = head - product(one_rows, mats, 0, one_rows)
    remain_rows = gather_row(remain_head)
    two_rows = gather_row(product(remain_rows, mats, 1, f_one))
    one_mine = lax.all_gather(half(one_rows, core, one_rows, one_rows), "col")
    two_mine = share(half(two_rows, core, f_two, one_mine), "col")
    mine = (one_mine, two_mine)
    other = [lax.ppermute(panel, "row", swap) for panel in mine]

    done = vectors.transpose(1, 0, 2).reshape(-1, k_all)
    for which, factor in enumerate((f_one, f_two)):
        done = update(done, factor, mine[which], other[which], core)
    solved, blocks = finish(done, one_mine, two_mine, lumped_mass, row // 2, col, (rounds, own, k_all))
    solved = solved.transpose(1, 0, 2)

    blocks = blocks.reshape((2, -1, BLOCK))
    there = lax.ppermute(lax.dynamic_index_in_dim(blocks, 1 - core, 0, keepdims=False), "row", swap)
    part = lax.dynamic_index_in_dim(blocks, core, 0, keepdims=False) + there
    part = exchange(part.reshape(cols_n, -1, BLOCK), "col").sum(axis=0)
    step = 2
    while step < rows_n:
        part = part + lax.ppermute(part, "row", [(i, i ^ step) for i in range(rows_n)])
        step *= 2
    mine = share(part, "col").reshape(-1, BLOCK, BLOCK)
    other = lax.ppermute(mine, "row", swap)

    inverse = inverse_factor(core, mine, other, k_all, 1.0 / ORDER)
    rotated = jnp.einsum("jtk,lk->jtl", solved, inverse, precision=HIGHEST, preferred_element_type=jnp.float32)
    return (solved, rotated)


def solution(mesh):
    placed = (
        P(("row", "col"), None, None),
        P("row", None, "col"),
        P("row", None, "col"),
        P(None, "row", "col"),
        P(("row", "col"), None),
    )
    return jax.shard_map(
        body,
        mesh=mesh,
        in_specs=placed,
        out_specs=(P(("row", "col"), None, None), P(("row", "col"), None, None)),
        check_vma=False,
    )
```

```python
import functools
import jax
import jax.numpy as jnp
from jax import lax
from jax.experimental import pallas as pl
from jax.experimental.pallas import tpu as pltpu
from jax.sharding import PartitionSpec as P

ORDER = 98304
HIGHEST = lax.Precision.HIGHEST


PIVOTS = 8
BLOCK = 128


def small_dot(a, b, a_dim, b_dim):
    return lax.dot_general(
        a, b, (((a_dim,), (b_dim,)), ((), ())), precision=HIGHEST, preferred_element_type=jnp.float32
    )


def identity(n):
    rows = lax.broadcasted_iota(jnp.int32, (n, n), 0)
    return jnp.where(rows == lax.broadcasted_iota(jnp.int32, (n, n), 1), 1.0, 0.0)


def invert_block(a_ref, b_ref):
    n = a_ref.shape[0]
    full = (PIVOTS, n)
    for lo in range(0, n, PIVOTS):
        block = a_ref[lo : lo + PIVOTS, :]
        other = b_ref[lo : lo + PIVOTS, :]
        d = {
            (i, j): jnp.broadcast_to(block[i : i + 1, lo + j : lo + j + 1], full)
            for i in range(PIVOTS)
            for j in range(i + 1)
        }
        a = [jnp.broadcast_to(block[j : j + 1, :], full) for j in range(PIVOTS)]
        b = [jnp.broadcast_to(other[j : j + 1, :], full) for j in range(PIVOTS)]
        r = {}
        for j in range(PIVOTS):
            r[j] = lax.rsqrt(d[j, j])
            for i in range(j + 1, PIVOTS):
                d[i, j] = d[i, j] * r[j]
            for i in range(j + 1, PIVOTS):
                for k in range(i, PIVOTS):
                    d[k, i] = d[k, i] - d[k, j] * d[i, j]
            a[j] = a[j] * r[j]
            b[j] = b[j] * r[j]
            for i in range(j + 1, PIVOTS):
                a[i] = a[i] - d[i, j] * a[j]
                b[i] = b[i] - d[i, j] * b[j]
        sub = lax.broadcasted_iota(jnp.int32, full, 0)
        done = b[0]
        for j in range(1, PIVOTS):
            done = jnp.where(sub == j, b[j], done)
        b_ref[lo : lo + PIVOTS, :] = done
        for at in range(lo + PIVOTS, n, PIVOTS):
            ah = a_ref[at : at + PIVOTS, :]
            bh = b_ref[at : at + PIVOTS, :]
            c = [jnp.broadcast_to(ah[:, lo + j : lo + j + 1], full) for j in range(PIVOTS)]
            for j in range(PIVOTS):
                c[j] = c[j] * r[j]
                for i in range(j + 1, PIVOTS):
                    c[i] = c[i] - d[i, j] * c[j]
                ah = ah - c[j] * a[j]
                bh = bh - c[j] * b[j]
            a_ref[at : at + PIVOTS, :] = ah
            b_ref[at : at + PIVOTS, :] = bh


def block_pairs(n):
    return [(i, j) for i in range(n // BLOCK) for j in range(i, n // BLOCK)]


def inverse_kernel(scale, core_ref, mine_ref, other_ref, out_ref, a_ref, s_ref, t_ref, u_ref):
    n = out_ref.shape[0]
    pairs = block_pairs(n)
    half = len(pairs) // 2
    core = core_ref[0]
    for side in range(2):
        for at, (i, j) in enumerate(pairs[side * half : (side + 1) * half]):
            rows, cols = slice(i * BLOCK, (i + 1) * BLOCK), slice(j * BLOCK, (j + 1) * BLOCK)
            part = jnp.where(core == side, mine_ref[at], other_ref[at])
            a_ref[rows, cols] = part * scale
    out_ref[...] = identity(n)

    def one(b, _):
        at = pl.multiple_of(b * BLOCK, BLOCK)
        rows = pl.ds(at, BLOCK)
        s_ref[...] = a_ref[rows, rows]
        t_ref[...] = identity(BLOCK)
        invert_block(s_ref, t_ref)
        inv = t_ref[...]
        below = lax.broadcasted_iota(jnp.int32, (BLOCK, n), 1) >= at + BLOCK
        u = small_dot(inv, jnp.where(below, a_ref[rows, :], 0.0), 1, 0)
        x = small_dot(inv, out_ref[rows, :], 1, 0)
        out_ref[rows, :] = x
        u_ref[...] = u

        def rest(i, _):
            later = pl.ds(pl.multiple_of(i * BLOCK, BLOCK), BLOCK)
            ui = u_ref[:, later]
            a_ref[later, :] = a_ref[later, :] - small_dot(ui, u, 0, 0)
            out_ref[later, :] = out_ref[later, :] - small_dot(ui, x, 0, 0)
            return 0

        lax.fori_loop(b + 1, n // BLOCK, rest, 0)
        return 0

    lax.fori_loop(0, n // BLOCK, one, 0)


def inverse_factor(core, mine, other, n, scale):
    return pl.pallas_call(
        functools.partial(inverse_kernel, scale),
        out_shape=jax.ShapeDtypeStruct((n, n), jnp.float32),
        in_specs=[pl.BlockSpec(memory_space=pltpu.SMEM)] + [pl.BlockSpec(memory_space=pltpu.VMEM)] * 2,
        out_specs=pl.BlockSpec(memory_space=pltpu.VMEM),
        scratch_shapes=[
            pltpu.VMEM((n, n), jnp.float32),
            pltpu.VMEM((BLOCK, BLOCK), jnp.float32),
            pltpu.VMEM((BLOCK, BLOCK), jnp.float32),
            pltpu.VMEM((BLOCK, n), jnp.float32),
        ],
        compiler_params=pltpu.CompilerParams(vmem_limit_bytes=16 * 1024 * 1024),
    )(jnp.full((1,), core, jnp.int32), mine, other)


def update_kernel(core_ref, start_ref, factor_ref, mine_ref, other_ref, out_ref):
    @pl.when(pl.program_id(0) == 0)
    def _():
        out_ref[...] = start_ref[...]

    chips, _, steps, own, _ = factor_ref.shape
    cols = out_ref.shape[1]
    lead = out_ref.shape[0] - steps * own
    f, p = [], []
    for ref, parity in ((mine_ref, core_ref[0]), (other_ref, 1 - core_ref[0])):
        for z in range(chips):
            f.append(factor_ref[z, parity].reshape(steps * own, BLOCK))
            p.append(ref[:, z].reshape(cols, BLOCK))
    out_ref[lead:, :] -= small_dot(jnp.concatenate(f, axis=1), jnp.concatenate(p, axis=1), 1, 1)


def update(start, factor, mine, other, core):
    chips = factor.shape[0]
    panel = pl.BlockSpec((mine.shape[0], 2) + mine.shape[2:], lambda s, p: (0, s, 0, 0))
    return pl.pallas_call(
        update_kernel,
        out_shape=jax.ShapeDtypeStruct(start.shape, jnp.float32),
        grid_spec=pltpu.PrefetchScalarGridSpec(
            num_scalar_prefetch=1,
            grid=(chips // 2,),
            in_specs=[
                pl.BlockSpec(start.shape, lambda s, p: (0, 0)),
                pl.BlockSpec((2,) + factor.shape[1:], lambda s, p: (s, 0, 0, 0, 0)),
                panel,
                panel,
            ],
            out_specs=pl.BlockSpec(start.shape, lambda s, p: (0, 0)),
        ),
        compiler_params=pltpu.CompilerParams(vmem_limit_bytes=56 * 1024 * 1024),
        cost_estimate=pl.CostEstimate(
            flops=24 * start.size * chips * BLOCK, bytes_accessed=24 * start.size, transcendentals=0
        ),
    )(jnp.full((1,), core, jnp.int32), start, factor, mine, other)


def finish_kernel(at_ref, update_ref, one_ref, two_ref, mass_ref, solved_ref, blocks_ref):
    rounds, own, k_all = solved_ref.shape
    lanes = lax.broadcasted_iota(jnp.int32, (own, BLOCK), 1)
    rows = lax.broadcasted_iota(jnp.int32, (own, BLOCK), 0)
    take = jnp.where(lanes == rows + at_ref[1] * own, 1.0, 0.0)
    for which, ref in enumerate((one_ref, two_ref)):
        solved_ref[which] = small_dot(take, ref[:, 0].reshape(k_all, BLOCK), 1, 1)
    solved_ref[2:] = update_ref[2 * own :, :].reshape(rounds - 2, own, k_all)
    all_rows = solved_ref[...].reshape(own * rounds, k_all)
    weighted = all_rows * mass_ref[...]
    at = 0
    for i in range(k_all // BLOCK):
        got = small_dot(weighted[:, i * BLOCK : (i + 1) * BLOCK], all_rows[:, i * BLOCK :], 0, 0)
        for j in range(k_all // BLOCK - i):
            blocks_ref[at] = got[:, j * BLOCK : (j + 1) * BLOCK]
            at += 1


def finish(updated, one, two, mass, place, col, shape):
    rounds, own, k_all = shape
    panel = pl.BlockSpec((one.shape[0], 1) + one.shape[2:], lambda s, at: (0, at[0], 0, 0))
    count = len(block_pairs(k_all))
    return pl.pallas_call(
        finish_kernel,
        out_shape=(
            jax.ShapeDtypeStruct(shape, jnp.float32),
            jax.ShapeDtypeStruct((count, BLOCK, BLOCK), jnp.float32),
        ),
        grid_spec=pltpu.PrefetchScalarGridSpec(
            num_scalar_prefetch=1,
            grid=(1,),
            in_specs=[
                pl.BlockSpec(updated.shape, lambda s, at: (0, 0)),
                panel,
                panel,
                pl.BlockSpec((own * rounds, 1), lambda s, at: (0, 0)),
            ],
            out_specs=(
                pl.BlockSpec(shape, lambda s, at: (0, 0, 0)),
                pl.BlockSpec((count, BLOCK, BLOCK), lambda s, at: (0, 0, 0)),
            ),
        ),
        compiler_params=pltpu.CompilerParams(vmem_limit_bytes=56 * 1024 * 1024),
        cost_estimate=pl.CostEstimate(flops=8 * updated.size * k_all, bytes_accessed=12 * updated.size, transcendentals=0),
    )(jnp.stack([place, col]).astype(jnp.int32), updated, one, two, mass.T.reshape(-1, 1))


def exchange(blocks, axis):
    return lax.all_to_all(blocks, axis, 0, 0)


def share(block, axis):
    size = lax.axis_size(axis)
    return exchange(jnp.broadcast_to(block[None], (size,) + block.shape), axis)


def gather_row(block):
    size = lax.axis_size("row")
    row = lax.axis_index("row")
    step, axis = size // 2, 0
    while step:
        got = lax.ppermute(block, "row", [(i, i ^ step) for i in range(size)])
        upper = (row & step) != 0
        block = jnp.stack([jnp.where(upper, got, block), jnp.where(upper, block, got)], axis=axis)
        step, axis = step // 2, axis + 1
    return block.reshape((size,) + block.shape[axis:])


def product_kernel(rows_ref, tiles_ref, after_ref, out_ref):
    count = rows_ref.shape[0]
    rows = jnp.concatenate([rows_ref[r] for r in range(count)], axis=1)
    tiles = jnp.concatenate([tiles_ref[r, 0] for r in range(count)], axis=1)
    out_ref[...] = small_dot(rows, tiles, 1, 1)


def product(rows, tiles, which, after):
    shape = (rows.shape[1], tiles.shape[2])
    return pl.pallas_call(
        product_kernel,
        out_shape=jax.ShapeDtypeStruct(shape, jnp.float32),
        grid=(1,),
        in_specs=[
            pl.BlockSpec(rows.shape, lambda s: (0, 0, 0)),
            pl.BlockSpec((tiles.shape[0], 1) + tiles.shape[2:], lambda s: (0, which, 0, 0)),
            pl.BlockSpec(memory_space=pl.ANY),
        ],
        out_specs=pl.BlockSpec(shape, lambda s: (0, 0)),
        compiler_params=pltpu.CompilerParams(vmem_limit_bytes=56 * 1024 * 1024),
        cost_estimate=pl.CostEstimate(
            flops=12 * rows.size * tiles.shape[2], bytes_accessed=4 * (rows.size + tiles.size // 2), transcendentals=0
        ),
    )(rows, tiles, after)


def hold_kernel(block_ref, after_ref, out_ref):
    out_ref[...] = block_ref[...]


def hold(block, after):
    return pl.pallas_call(
        hold_kernel,
        out_shape=jax.ShapeDtypeStruct(block.shape, block.dtype),
        in_specs=[pl.BlockSpec(memory_space=pltpu.VMEM), pl.BlockSpec(memory_space=pl.ANY)],
        out_specs=pl.BlockSpec(memory_space=pltpu.VMEM),
        cost_estimate=pl.CostEstimate(flops=0, bytes_accessed=8 * block.size, transcendentals=0),
    )(block, after)


def keep_kernel(block_ref, after_ref, out_ref):
    pass


def keep(block, after):
    return pl.pallas_call(
        keep_kernel,
        out_shape=jax.ShapeDtypeStruct(block.shape, block.dtype),
        in_specs=[pl.BlockSpec(memory_space=pl.ANY)] * 2,
        out_specs=pl.BlockSpec(memory_space=pl.ANY),
        input_output_aliases={0: 0},
        compiler_params=pltpu.CompilerParams(vmem_limit_bytes=56 * 1024 * 1024),
    )(block, after)


def half_kernel(core_ref, panel_ref, after_ref, out_ref):
    out_ref[...] = panel_ref[:, 0]


def half(panel, core, after):
    pairs = (panel.shape[0] // 2, 2) + panel.shape[1:]
    shape = (pairs[0],) + pairs[2:]
    return pl.pallas_call(
        half_kernel,
        out_shape=jax.ShapeDtypeStruct(shape, jnp.float32),
        grid_spec=pltpu.PrefetchScalarGridSpec(
            num_scalar_prefetch=1,
            grid=(1,),
            in_specs=[pl.BlockSpec((pairs[0], 1) + pairs[2:], lambda s, p: (0, p[0], 0, 0)), pl.BlockSpec(memory_space=pl.ANY)],
            out_specs=pl.BlockSpec(shape, lambda s, p: (0, 0, 0)),
        ),
        compiler_params=pltpu.CompilerParams(vmem_limit_bytes=56 * 1024 * 1024),
        cost_estimate=pl.CostEstimate(flops=0, bytes_accessed=4 * panel.size, transcendentals=0),
    )(jnp.full((1,), core, jnp.int32), panel.reshape(pairs), after)


def body(vectors, factor_one, factor_two, block_inverse, lumped_mass):
    rows_n, cols_n = lax.axis_size("row"), lax.axis_size("col")
    row, col = lax.axis_index("row"), lax.axis_index("col")
    core = row % 2
    own, rounds, k_all = vectors.shape
    tile = own * cols_n
    k_part = k_all // cols_n
    swap = [(i, i ^ 1) for i in range(rows_n)]
    turn = [(r * cols_n + c, c * cols_n + r) for r in range(rows_n) for c in range(cols_n)]

    stack = jnp.stack([factor_one[:, 0, :], block_inverse[1]])
    mats = lax.all_gather(stack, "col")

    turned = lax.ppermute(hold(vectors[:, 0, :], stack), ("row", "col"), turn)
    block = gather_row(turned).reshape(tile, k_all)
    parts = jnp.einsum("qk,iq->ki", block, block_inverse[0], precision=HIGHEST, preferred_element_type=jnp.float32)
    head = vectors[:, 1, :].reshape(own, cols_n, k_part).transpose(1, 0, 2).reshape(cols_n, -1, BLOCK)
    head_rows = head.shape[1]
    head = jnp.pad(head, ((0, 0), (0, own - head_rows), (0, 0)))
    both = exchange(jnp.concatenate([parts.reshape(cols_n, k_part, tile), head], axis=1), "col")
    one = both[:, :k_part].sum(axis=0)
    head = both[:, k_part : k_part + head_rows].reshape(cols_n, own, k_part)
    head = head.transpose(2, 0, 1).reshape(k_part, tile)

    def redistribute(factor):
        parts = factor.reshape((cols_n, own) + factor.shape[1:]).transpose(0, 2, 1, 3)
        parts = exchange(parts, "col")
        return parts.reshape((rows_n // 2, 2) + parts.shape[1:])

    one_rows = gather_row(hold(one, mats))
    f_one = redistribute(factor_one)
    f_two = redistribute(factor_two)
    remain_head = head - product(one_rows, mats, 0, one_rows)
    remain_rows = gather_row(remain_head)
    two_rows = gather_row(product(remain_rows, mats, 1, f_one))
    one_mine = lax.all_gather(half(one_rows, core, one_rows), "col")
    two_half = half(two_rows, core, f_two)
    one_mine = keep(one_mine, two_half)
    two_mine = share(two_half, "col")
    done = vectors.transpose(1, 0, 2).reshape(-1, k_all)
    done = update(done, f_one, one_mine, lax.ppermute(one_mine, "row", swap), core)
    two_mine = keep(two_mine, done)
    done = update(done, f_two, two_mine, lax.ppermute(two_mine, "row", swap), core)
    solved, blocks = finish(done, one_mine, two_mine, lumped_mass, row // 2, col, (rounds, own, k_all))
    solved = solved.transpose(1, 0, 2)

    blocks = blocks.reshape((2, -1, BLOCK))
    there = lax.ppermute(lax.dynamic_index_in_dim(blocks, 1 - core, 0, keepdims=False), "row", swap)
    part = lax.dynamic_index_in_dim(blocks, core, 0, keepdims=False) + there
    part = exchange(part.reshape(cols_n, -1, BLOCK), "col").sum(axis=0)
    step = 2
    while step < rows_n:
        part = part + lax.ppermute(part, "row", [(i, i ^ step) for i in range(rows_n)])
        step *= 2
    mine = share(part, "col").reshape(-1, BLOCK, BLOCK)
    other = lax.ppermute(mine, "row", swap)

    inverse = inverse_factor(core, mine, other, k_all, 1.0 / ORDER)
    rotated = jnp.einsum("jtk,lk->jtl", solved, inverse, precision=HIGHEST, preferred_element_type=jnp.float32)
    return (solved, rotated)


def solution(mesh):
    placed = (
        P(("row", "col"), None, None),
        P("row", None, "col"),
        P("row", None, "col"),
        P(None, "row", "col"),
        P(("row", "col"), None),
    )
    return jax.shard_map(
        body,
        mesh=mesh,
        in_specs=placed,
        out_specs=(P(("row", "col"), None, None), P(("row", "col"), None, None)),
        check_vma=False,
    )
```

```python
import functools
import jax
import jax.numpy as jnp
from jax import lax
from jax.experimental import pallas as pl
from jax.experimental.pallas import tpu as pltpu
from jax.sharding import PartitionSpec as P

ORDER = 98304
HIGHEST = lax.Precision.HIGHEST


PIVOTS = 8
BLOCK = 128


def small_dot(a, b, a_dim, b_dim):
    return lax.dot_general(
        a, b, (((a_dim,), (b_dim,)), ((), ())), precision=HIGHEST, preferred_element_type=jnp.float32
    )


def identity(n):
    rows = lax.broadcasted_iota(jnp.int32, (n, n), 0)
    return jnp.where(rows == lax.broadcasted_iota(jnp.int32, (n, n), 1), 1.0, 0.0)


def invert_block(a_ref, b_ref):
    n = a_ref.shape[0]
    full = (PIVOTS, n)
    for lo in range(0, n, PIVOTS):
        block = a_ref[lo : lo + PIVOTS, :]
        other = b_ref[lo : lo + PIVOTS, :]
        d = {
            (i, j): jnp.broadcast_to(block[i : i + 1, lo + j : lo + j + 1], full)
            for i in range(PIVOTS)
            for j in range(i + 1)
        }
        a = [jnp.broadcast_to(block[j : j + 1, :], full) for j in range(PIVOTS)]
        b = [jnp.broadcast_to(other[j : j + 1, :], full) for j in range(PIVOTS)]
        r = {}
        for j in range(PIVOTS):
            r[j] = lax.rsqrt(d[j, j])
            for i in range(j + 1, PIVOTS):
                d[i, j] = d[i, j] * r[j]
            for i in range(j + 1, PIVOTS):
                for k in range(i, PIVOTS):
                    d[k, i] = d[k, i] - d[k, j] * d[i, j]
            a[j] = a[j] * r[j]
            b[j] = b[j] * r[j]
            for i in range(j + 1, PIVOTS):
                a[i] = a[i] - d[i, j] * a[j]
                b[i] = b[i] - d[i, j] * b[j]
        sub = lax.broadcasted_iota(jnp.int32, full, 0)
        done = b[0]
        for j in range(1, PIVOTS):
            done = jnp.where(sub == j, b[j], done)
        b_ref[lo : lo + PIVOTS, :] = done
        for at in range(lo + PIVOTS, n, PIVOTS):
            ah = a_ref[at : at + PIVOTS, :]
            bh = b_ref[at : at + PIVOTS, :]
            c = [jnp.broadcast_to(ah[:, lo + j : lo + j + 1], full) for j in range(PIVOTS)]
            for j in range(PIVOTS):
                c[j] = c[j] * r[j]
                for i in range(j + 1, PIVOTS):
                    c[i] = c[i] - d[i, j] * c[j]
                ah = ah - c[j] * a[j]
                bh = bh - c[j] * b[j]
            a_ref[at : at + PIVOTS, :] = ah
            b_ref[at : at + PIVOTS, :] = bh


def block_pairs(n):
    return [(i, j) for i in range(n // BLOCK) for j in range(i, n // BLOCK)]


def inverse_kernel(scale, core_ref, mine_ref, other_ref, out_ref, a_ref, s_ref, t_ref, u_ref):
    n = out_ref.shape[0]
    pairs = block_pairs(n)
    half = len(pairs) // 2
    core = core_ref[0]
    for side in range(2):
        for at, (i, j) in enumerate(pairs[side * half : (side + 1) * half]):
            rows, cols = slice(i * BLOCK, (i + 1) * BLOCK), slice(j * BLOCK, (j + 1) * BLOCK)
            part = jnp.where(core == side, mine_ref[at], other_ref[at])
            a_ref[rows, cols] = part * scale
    out_ref[...] = identity(n)

    def one(b, _):
        at = pl.multiple_of(b * BLOCK, BLOCK)
        rows = pl.ds(at, BLOCK)
        s_ref[...] = a_ref[rows, rows]
        t_ref[...] = identity(BLOCK)
        invert_block(s_ref, t_ref)
        inv = t_ref[...]
        below = lax.broadcasted_iota(jnp.int32, (BLOCK, n), 1) >= at + BLOCK
        u = small_dot(inv, jnp.where(below, a_ref[rows, :], 0.0), 1, 0)
        x = small_dot(inv, out_ref[rows, :], 1, 0)
        out_ref[rows, :] = x
        u_ref[...] = u

        def rest(i, _):
            later = pl.ds(pl.multiple_of(i * BLOCK, BLOCK), BLOCK)
            ui = u_ref[:, later]
            a_ref[later, :] = a_ref[later, :] - small_dot(ui, u, 0, 0)
            out_ref[later, :] = out_ref[later, :] - small_dot(ui, x, 0, 0)
            return 0

        lax.fori_loop(b + 1, n // BLOCK, rest, 0)
        return 0

    lax.fori_loop(0, n // BLOCK, one, 0)


def inverse_factor(core, mine, other, n, scale):
    return pl.pallas_call(
        functools.partial(inverse_kernel, scale),
        out_shape=jax.ShapeDtypeStruct((n, n), jnp.float32),
        in_specs=[pl.BlockSpec(memory_space=pltpu.SMEM)] + [pl.BlockSpec(memory_space=pltpu.VMEM)] * 2,
        out_specs=pl.BlockSpec(memory_space=pltpu.VMEM),
        scratch_shapes=[
            pltpu.VMEM((n, n), jnp.float32),
            pltpu.VMEM((BLOCK, BLOCK), jnp.float32),
            pltpu.VMEM((BLOCK, BLOCK), jnp.float32),
            pltpu.VMEM((BLOCK, n), jnp.float32),
        ],
        compiler_params=pltpu.CompilerParams(vmem_limit_bytes=16 * 1024 * 1024),
    )(jnp.full((1,), core, jnp.int32), mine, other)


def update_kernel(core_ref, start_ref, factor_ref, mine_ref, other_ref, out_ref):
    @pl.when(pl.program_id(0) == 0)
    def _():
        out_ref[...] = start_ref[...]

    chips, _, steps, own, _ = factor_ref.shape
    cols = out_ref.shape[1]
    lead = out_ref.shape[0] - steps * own
    f, p = [], []
    for ref, parity in ((mine_ref, core_ref[0]), (other_ref, 1 - core_ref[0])):
        for z in range(chips):
            f.append(factor_ref[z, parity].reshape(steps * own, BLOCK))
            p.append(ref[:, z].reshape(cols, BLOCK))
    out_ref[lead:, :] -= small_dot(jnp.concatenate(f, axis=1), jnp.concatenate(p, axis=1), 1, 1)


def update(start, factor, mine, other, core):
    chips = factor.shape[0]
    panel = pl.BlockSpec((mine.shape[0], 2) + mine.shape[2:], lambda s, p: (0, s, 0, 0))
    return pl.pallas_call(
        update_kernel,
        out_shape=jax.ShapeDtypeStruct(start.shape, jnp.float32),
        grid_spec=pltpu.PrefetchScalarGridSpec(
            num_scalar_prefetch=1,
            grid=(chips // 2,),
            in_specs=[
                pl.BlockSpec(start.shape, lambda s, p: (0, 0)),
                pl.BlockSpec((2,) + factor.shape[1:], lambda s, p: (s, 0, 0, 0, 0)),
                panel,
                panel,
            ],
            out_specs=pl.BlockSpec(start.shape, lambda s, p: (0, 0)),
        ),
        compiler_params=pltpu.CompilerParams(vmem_limit_bytes=56 * 1024 * 1024),
        cost_estimate=pl.CostEstimate(
            flops=24 * start.size * chips * BLOCK, bytes_accessed=24 * start.size, transcendentals=0
        ),
    )(jnp.full((1,), core, jnp.int32), start, factor, mine, other)


def finish_kernel(at_ref, update_ref, one_ref, two_ref, mass_ref, solved_ref, mine_ref, there_ref):
    rounds, own, k_all = solved_ref.shape
    lanes = lax.broadcasted_iota(jnp.int32, (own, BLOCK), 1)
    rows = lax.broadcasted_iota(jnp.int32, (own, BLOCK), 0)
    take = jnp.where(lanes == rows + at_ref[1] * own, 1.0, 0.0)
    for which, ref in enumerate((one_ref, two_ref)):
        solved_ref[which] = small_dot(take, ref[:, 0].reshape(k_all, BLOCK), 1, 1)
    solved_ref[2:] = update_ref[2 * own :, :].reshape(rounds - 2, own, k_all)
    all_rows = solved_ref[...].reshape(own * rounds, k_all)
    weighted = all_rows * mass_ref[...]
    at = 0
    for i in range(k_all // BLOCK):
        got = small_dot(weighted[:, i * BLOCK : (i + 1) * BLOCK], all_rows[:, i * BLOCK :], 0, 0)
        for j in range(k_all // BLOCK - i):
            side, place = at // mine_ref.shape[0], at % mine_ref.shape[0]
            part = got[:, j * BLOCK : (j + 1) * BLOCK]

            @pl.when(at_ref[2] == side)
            def _():
                mine_ref[place] = part

            @pl.when(at_ref[2] != side)
            def _():
                there_ref[place] = part

            at += 1


def finish(updated, one, two, mass, place, col, core, shape):
    rounds, own, k_all = shape
    panel = pl.BlockSpec((one.shape[0], 1) + one.shape[2:], lambda s, at: (0, at[0], 0, 0))
    count = len(block_pairs(k_all)) // 2
    return pl.pallas_call(
        finish_kernel,
        out_shape=(
            jax.ShapeDtypeStruct(shape, jnp.float32),
            jax.ShapeDtypeStruct((count, BLOCK, BLOCK), jnp.float32),
            jax.ShapeDtypeStruct((count, BLOCK, BLOCK), jnp.float32),
        ),
        grid_spec=pltpu.PrefetchScalarGridSpec(
            num_scalar_prefetch=1,
            grid=(1,),
            in_specs=[
                pl.BlockSpec(updated.shape, lambda s, at: (0, 0)),
                panel,
                panel,
                pl.BlockSpec((own * rounds, 1), lambda s, at: (0, 0)),
            ],
            out_specs=(
                pl.BlockSpec(shape, lambda s, at: (0, 0, 0)),
                pl.BlockSpec((count, BLOCK, BLOCK), lambda s, at: (0, 0, 0)),
                pl.BlockSpec((count, BLOCK, BLOCK), lambda s, at: (0, 0, 0)),
            ),
        ),
        compiler_params=pltpu.CompilerParams(vmem_limit_bytes=56 * 1024 * 1024),
        cost_estimate=pl.CostEstimate(flops=8 * updated.size * k_all, bytes_accessed=12 * updated.size, transcendentals=0),
    )(jnp.stack([place, col, core]).astype(jnp.int32), updated, one, two, mass.T.reshape(-1, 1))


def exchange(blocks, axis):
    return lax.all_to_all(blocks, axis, 0, 0)


def share(block, axis):
    size = lax.axis_size(axis)
    return exchange(jnp.broadcast_to(block[None], (size,) + block.shape), axis)


def gather_row(block):
    size = lax.axis_size("row")
    row = lax.axis_index("row")
    step, axis = size // 2, 0
    while step:
        got = lax.ppermute(block, "row", [(i, i ^ step) for i in range(size)])
        upper = (row & step) != 0
        block = jnp.stack([jnp.where(upper, got, block), jnp.where(upper, block, got)], axis=axis)
        step, axis = step // 2, axis + 1
    return block.reshape((size,) + block.shape[axis:])


def product_kernel(rows_ref, tiles_ref, after_ref, out_ref):
    count = rows_ref.shape[0]
    rows = jnp.concatenate([rows_ref[r] for r in range(count)], axis=1)
    tiles = jnp.concatenate([tiles_ref[r, 0] for r in range(count)], axis=1)
    out_ref[...] = small_dot(rows, tiles, 1, 1)


def product(rows, tiles, which, after):
    shape = (rows.shape[1], tiles.shape[2])
    return pl.pallas_call(
        product_kernel,
        out_shape=jax.ShapeDtypeStruct(shape, jnp.float32),
        grid=(1,),
        in_specs=[
            pl.BlockSpec(rows.shape, lambda s: (0, 0, 0)),
            pl.BlockSpec((tiles.shape[0], 1) + tiles.shape[2:], lambda s: (0, which, 0, 0)),
            pl.BlockSpec(memory_space=pl.ANY),
        ],
        out_specs=pl.BlockSpec(shape, lambda s: (0, 0)),
        compiler_params=pltpu.CompilerParams(vmem_limit_bytes=56 * 1024 * 1024),
        cost_estimate=pl.CostEstimate(
            flops=12 * rows.size * tiles.shape[2], bytes_accessed=4 * (rows.size + tiles.size // 2), transcendentals=0
        ),
    )(rows, tiles, after)


def hold_kernel(block_ref, after_ref, out_ref):
    out_ref[...] = block_ref[...]


def hold(block, after):
    return pl.pallas_call(
        hold_kernel,
        out_shape=jax.ShapeDtypeStruct(block.shape, block.dtype),
        in_specs=[pl.BlockSpec(memory_space=pltpu.VMEM), pl.BlockSpec(memory_space=pl.ANY)],
        out_specs=pl.BlockSpec(memory_space=pltpu.VMEM),
        cost_estimate=pl.CostEstimate(flops=0, bytes_accessed=8 * block.size, transcendentals=0),
    )(block, after)


def keep_kernel(block_ref, after_ref, out_ref):
    pass


def keep(block, after):
    return pl.pallas_call(
        keep_kernel,
        out_shape=jax.ShapeDtypeStruct(block.shape, block.dtype),
        in_specs=[pl.BlockSpec(memory_space=pl.ANY)] * 2,
        out_specs=pl.BlockSpec(memory_space=pl.ANY),
        input_output_aliases={0: 0},
        compiler_params=pltpu.CompilerParams(vmem_limit_bytes=56 * 1024 * 1024),
    )(block, after)


def half_kernel(core_ref, panel_ref, after_ref, out_ref):
    out_ref[...] = panel_ref[:, 0]


def half(panel, core, after):
    pairs = (panel.shape[0] // 2, 2) + panel.shape[1:]
    shape = (pairs[0],) + pairs[2:]
    return pl.pallas_call(
        half_kernel,
        out_shape=jax.ShapeDtypeStruct(shape, jnp.float32),
        grid_spec=pltpu.PrefetchScalarGridSpec(
            num_scalar_prefetch=1,
            grid=(1,),
            in_specs=[pl.BlockSpec((pairs[0], 1) + pairs[2:], lambda s, p: (0, p[0], 0, 0)), pl.BlockSpec(memory_space=pl.ANY)],
            out_specs=pl.BlockSpec(shape, lambda s, p: (0, 0, 0)),
        ),
        compiler_params=pltpu.CompilerParams(vmem_limit_bytes=56 * 1024 * 1024),
        cost_estimate=pl.CostEstimate(flops=0, bytes_accessed=4 * panel.size, transcendentals=0),
    )(jnp.full((1,), core, jnp.int32), panel.reshape(pairs), after)


def body(vectors, factor_one, factor_two, block_inverse, lumped_mass):
    rows_n, cols_n = lax.axis_size("row"), lax.axis_size("col")
    row, col = lax.axis_index("row"), lax.axis_index("col")
    core = row % 2
    own, rounds, k_all = vectors.shape
    tile = own * cols_n
    k_part = k_all // cols_n
    swap = [(i, i ^ 1) for i in range(rows_n)]
    turn = [(r * cols_n + c, c * cols_n + r) for r in range(rows_n) for c in range(cols_n)]

    stack = jnp.stack([factor_one[:, 0, :], block_inverse[1]])
    mats = lax.all_gather(stack, "col")

    turned = lax.ppermute(hold(vectors[:, 0, :], stack), ("row", "col"), turn)
    block = gather_row(turned).reshape(tile, k_all)
    parts = jnp.einsum("qk,iq->ki", block, block_inverse[0], precision=HIGHEST, preferred_element_type=jnp.float32)
    head = vectors[:, 1, :].reshape(own, cols_n, k_part).transpose(1, 0, 2).reshape(cols_n, -1, BLOCK)
    head_rows = head.shape[1]
    head = jnp.pad(head, ((0, 0), (0, own - head_rows), (0, 0)))
    both = exchange(jnp.concatenate([parts.reshape(cols_n, k_part, tile), head], axis=1), "col")
    one = both[:, :k_part].sum(axis=0)
    head = both[:, k_part : k_part + head_rows].reshape(cols_n, own, k_part)
    head = head.transpose(2, 0, 1).reshape(k_part, tile)

    def redistribute(factor):
        parts = factor.reshape((cols_n, own) + factor.shape[1:]).transpose(0, 2, 1, 3)
        parts = exchange(parts, "col")
        return parts.reshape((rows_n // 2, 2) + parts.shape[1:])

    one_rows = gather_row(hold(one, mats))
    f_one = redistribute(factor_one)
    f_two = redistribute(factor_two)
    remain_head = head - product(one_rows, mats, 0, one_rows)
    remain_rows = gather_row(remain_head)
    two_rows = gather_row(product(remain_rows, mats, 1, f_one))
    one_mine = lax.all_gather(half(one_rows, core, one_rows), "col")
    two_half = half(two_rows, core, f_two)
    one_mine = keep(one_mine, two_half)
    two_mine = share(two_half, "col")
    done = vectors.transpose(1, 0, 2).reshape(-1, k_all)
    done = update(done, f_one, one_mine, lax.ppermute(one_mine, "row", swap), core)
    two_mine = keep(two_mine, done)
    done = update(done, f_two, two_mine, lax.ppermute(two_mine, "row", swap), core)
    solved, kept, given = finish(done, one_mine, two_mine, lumped_mass, row // 2, col, core, (rounds, own, k_all))
    solved = solved.transpose(1, 0, 2)

    part = kept + lax.ppermute(given, "row", swap)
    part = exchange(part.reshape(cols_n, -1, BLOCK), "col").sum(axis=0)
    step = 2
    while step < rows_n:
        part = part + lax.ppermute(part, "row", [(i, i ^ step) for i in range(rows_n)])
        step *= 2
    mine = share(part, "col").reshape(-1, BLOCK, BLOCK)
    other = lax.ppermute(mine, "row", swap)

    inverse = inverse_factor(core, mine, other, k_all, 1.0 / ORDER)
    rotated = jnp.einsum("jtk,lk->jtl", solved, inverse, precision=HIGHEST, preferred_element_type=jnp.float32)
    return (solved, rotated)


def solution(mesh):
    placed = (
        P(("row", "col"), None, None),
        P("row", None, "col"),
        P("row", None, "col"),
        P(None, "row", "col"),
        P(("row", "col"), None),
    )
    return jax.shard_map(
        body,
        mesh=mesh,
        in_specs=placed,
        out_specs=(P(("row", "col"), None, None), P(("row", "col"), None, None)),
        check_vma=False,
    )
```
